256 devices in a mesh: dp: 8 (over z), dap: 32 (over y, x, core).
Axes of the slice: x: 4, y: 4, z: 8, core: 2. Of those that a mesh axis runs over, the one named last changes fastest.
Arguments:
- pair_repr: bfloat16 [8, 256, 256, 128], P('dp', 'dap'), may hold values from -6 to 6
- lengths: int32 [8], P('dp'), may hold values from 128 to 256, as said below
- tri_project: bfloat16 [128, 512], P('dp'), may hold values from -0.5 to 0.5
- tri_gate: bfloat16 [128, 128], P('dp'), may hold values from -0.5 to 0.5
- tri_output: bfloat16 [128, 128], P('dp'), may hold values from -0.5 to 0.5
- attn_project: bfloat16 [128, 512], P('dp'), may hold values from -0.5 to 0.5
- attn_bias: bfloat16 [128, 4], P('dp'), may hold values from -60 to 60
- attn_output: bfloat16 [128, 128], P('dp'), may hold values from -0.5 to 0.5
- trans_expand: bfloat16 [128, 1024], P('dp'), may hold values from -0.5 to 0.5
- trans_reduce: bfloat16 [512, 128], P('dp'), may hold values from -0.25 to 0.25
Outputs:
- pair_out: bfloat16 [8, 256, 256, 128], P('dp', 'dap')
The draws below stay inside these ranges and needn't reach their ends.
Inputs may be any that keep to these rules, and one draw needn't show every extreme that they name: `lengths`: at least one complex has exactly 256 tokens.
All inputs are finite; a program needn't handle non-finite values.
Results may differ from the reference program's by a relative error of at most 0.04.
Values may be sent and summed in bfloat16 or wider, within the bound.
A program may use at most 128 MiB of HBM per device.

```python
import jax
import jax.numpy as jnp
from jax import lax

C = 128
H = 4
NMAX = 256
FF = 512
COMPLEXES = 8


def draw_lengths(key, part):
    key = jax.random.fold_in(key, 1)
    first_key, second_key = jax.random.split(key)
    drawn = jax.random.randint(first_key, (COMPLEXES,), NMAX // 2, NMAX + 1)
    longest = jax.random.randint(second_key, (), 0, COMPLEXES)
    return drawn.at[longest].set(NMAX).astype(jnp.int32)


def draw_attn_bias(key, part):
    key = jax.random.fold_in(key, 2)
    first_key, second_key = jax.random.split(key)
    scales = jnp.exp(jax.random.uniform(first_key, (H,), jnp.float32, 0.0, jnp.log(8.0)))
    values = jax.random.normal(second_key, (C, H), jnp.float32) * scales[None, :] / C ** 0.5
    return jnp.clip(values, -60.0, 60.0).astype(jnp.bfloat16)


def levels(own_key, shape, cuts, low, top_value):
    factor_of = 1.0
    for dim, shards_of in cuts:
        draws = jax.random.uniform(jax.random.fold_in(jax.random.fold_in(own_key, 6), dim), (shards_of,), jnp.float32, low / len(cuts), top_value / len(cuts))
        factor_of = factor_of * jnp.repeat(jnp.exp(draws), shape[dim] // shards_of).reshape((-1,) + (1,) * (len(shape) - 1 - dim))
    return factor_of


def bell_draw(own_key, extent, scale, reach, shards=(), held_as=jnp.bfloat16):
    result = jax.random.normal(own_key, extent, jnp.float32) * scale
    if len(shards) > 0:
        result = levels(own_key, extent, shards, -0.22, 0.18) * result
    return jnp.clip(result, min=-reach, max=reach).astype(held_as)


def setup_inputs(seed: int = 0) -> dict:
    splits = jax.random.split(jax.random.key(seed), 11)
    return {
        "pair_repr": bell_draw(splits[0], (COMPLEXES, NMAX, NMAX, C), 1.0, 6.0, ((0, 8), (1, 32))),
        "lengths": draw_lengths(jax.random.fold_in(splits[10], 71), 0),
        "tri_project": bell_draw(splits[2], (C, 4 * C), C ** -0.5, 0.5, ((0, 8),)),
        "tri_gate": bell_draw(splits[3], (C, C), C ** -0.5, 0.5, ((0, 8),)),
        "tri_output": bell_draw(splits[4], (C, C), C ** -0.5, 0.5, ((0, 8),)),
        "attn_project": bell_draw(splits[5], (C, 4 * C), C ** -0.5, 0.5, ((0, 8),)),
        "attn_bias": draw_attn_bias(jax.random.fold_in(splits[10], 71), 0),
        "attn_output": bell_draw(splits[7], (C, C), C ** -0.5, 0.5, ((0, 8),)),
        "trans_expand": bell_draw(splits[8], (C, 2 * FF), C ** -0.5, 0.5, ((0, 8),)),
        "trans_reduce": bell_draw(splits[9], (FF, C), FF ** -0.5, 0.25, ((0, 8),)),
    }


def layer_norm(values):
    mean = lax.optimization_barrier(jnp.mean(values, axis=-1, keepdims=True))
    centred = values - mean
    variance = lax.optimization_barrier(jnp.mean(centred * centred, axis=-1, keepdims=True))
    return centred * lax.rsqrt(variance + 1e-05)

def matmul(left, right):
    shape = left.shape
    flat = left.reshape(-1, shape[-1])
    return jnp.dot(flat, right, preferred_element_type=jnp.float32).reshape(shape[:-1] + (right.shape[1],))

def one_complex(pair_one, length, tri_project, tri_gate, tri_output, attn_project, attn_bias, attn_output, trans_expand, trans_reduce):
    token_count = pair_one.shape[0]
    channels = pair_one.shape[2]
    head_count = attn_bias.shape[1]
    head_size = channels // head_count
    valid = (jnp.arange(token_count) < length).astype(jnp.float32)
    pair_mask = valid[:, None] * valid[None, :]
    pair_in = pair_one.astype(jnp.float32)
    normed = layer_norm(pair_in).astype(jnp.bfloat16)
    projected = matmul(normed, tri_project)
    left_proj = (jax.nn.sigmoid(projected[..., :channels]) * projected[..., channels:2 * channels] * pair_mask[..., None]).astype(jnp.bfloat16)
    right_proj = (jax.nn.sigmoid(projected[..., 2 * channels:3 * channels]) * projected[..., 3 * channels:] * pair_mask[..., None]).astype(jnp.bfloat16)
    gate_out = jax.nn.sigmoid(matmul(normed, tri_gate))
    contracted = jnp.einsum('ikc,jkc->ijc', left_proj.astype(jnp.float32), right_proj.astype(jnp.float32))
    contracted_norm = layer_norm(contracted).astype(jnp.bfloat16)
    first = pair_in + gate_out * matmul(contracted_norm, tri_output)
    first_norm = layer_norm(first).astype(jnp.bfloat16)
    attn_all = matmul(first_norm, attn_project)
    queries = attn_all[..., :channels].astype(jnp.bfloat16).reshape(token_count, token_count, head_count, head_size)
    keys_all = attn_all[..., channels:2 * channels].astype(jnp.bfloat16).reshape(token_count, token_count, head_count, head_size)
    values_all = attn_all[..., 2 * channels:3 * channels].astype(jnp.bfloat16).reshape(token_count, token_count, head_count, head_size)
    gates = attn_all[..., 3 * channels:].astype(jnp.bfloat16)
    bias_pair = matmul(first_norm, attn_bias).astype(jnp.bfloat16)
    bias_ik = jnp.transpose(bias_pair, (2, 1, 0)).astype(jnp.float32)
    inv_sqrt = 1.0 / head_size ** 0.5

    def column_attend(column):
        query_col = queries[:, column].astype(jnp.float32)
        key_col = keys_all[:, column].astype(jnp.float32)
        value_col = values_all[:, column].astype(jnp.float32)
        scores = jnp.einsum('ihd,khd->hik', query_col, key_col) * inv_sqrt + bias_ik
        scores = jnp.where(valid[None, None, :] > 0, scores, -1000000000.0)
        soft = jax.nn.softmax(scores, axis=-1).astype(jnp.bfloat16)
        attended = jnp.einsum('hik,khd->ihd', soft.astype(jnp.float32), value_col)
        return attended.reshape(token_count, channels)
    attended = lax.map(column_attend, jnp.arange(token_count))
    attended = jnp.transpose(attended, (1, 0, 2))
    gated_out = (jax.nn.sigmoid(gates.astype(jnp.float32)) * attended).astype(jnp.bfloat16)
    second = first + matmul(gated_out, attn_output)
    second_norm = layer_norm(second).astype(jnp.bfloat16)
    expanded = matmul(second_norm, trans_expand)
    hidden_units = trans_reduce.shape[0]
    activated = (jax.nn.silu(expanded[..., :hidden_units]) * expanded[..., hidden_units:]).astype(jnp.bfloat16)
    return (second + matmul(activated, trans_reduce)).astype(jnp.bfloat16)

def reference(pair_repr, lengths, tri_project, tri_gate, tri_output, attn_project, attn_bias, attn_output, trans_expand, trans_reduce):
    results = []
    for member in range(pair_repr.shape[0]):
        results.append(one_complex(pair_repr[member], lengths[member], tri_project, tri_gate, tri_output, attn_project, attn_bias, attn_output, trans_expand, trans_reduce))
    return jnp.stack(results, axis=0)
```

```python
import functools

import jax
import jax.numpy as jnp
from jax import lax
from jax.experimental import pallas as pl
from jax.experimental.pallas import tpu as pltpu
from jax.sharding import PartitionSpec as P

F32 = jnp.float32
BF16 = jnp.bfloat16
NN = (((1,), (0,)), ((), ()))
NT = (((1,), (1,)), ((), ()))
TN = (((0,), (0,)), ((), ()))
LOG2E = 1.4426950408889634
EPS = 1e-05

ROWS = 8
TOKENS = 256
C = 128
HEADS = 4
HEAD = 32
FF = 512
DAP = TOKENS // ROWS
HALF = C // 2


def dot(left, right, dims):
    return lax.dot_general(left, right, dims, preferred_element_type=F32)


def sigmoid(v):
    return 0.5 + 0.5 * jnp.tanh(0.5 * v)


def norm_over(values, axis):
    mean = jnp.mean(values, axis=axis, keepdims=True)
    centred = values - mean
    variance = jnp.mean(centred * centred, axis=axis, keepdims=True)
    return centred * lax.rsqrt(variance + EPS)


def transposed(value):
    return jnp.transpose(value.astype(F32)).astype(BF16)


def wait_bytes(ref, sem):
    pltpu.make_async_copy(ref, ref, sem).wait()


def body(
    dp_count,
    length_ref,
    x_ref,
    tri_project_ref,
    tri_gate_ref,
    tri_output_ref,
    attn_project_ref,
    attn_bias_ref,
    attn_output_ref,
    expand_ref,
    reduce_ref,
    out_ref,
    mix_stage,
    w_tri,
    w_mix,
    w_expand,
    w_reduce,
    wt_tri,
    wt_mix,
    wt_expand,
    wt_reduce,
    pair_stage,
    pair_recv,
    normed_rows,
    lr_rows,
    lr_stage,
    lr_recv,
    c_stage,
    c_recv,
    c_normed,
    x_cols,
    xt,
    gate_t,
    first_t,
    first_norm_t,
    bias_rows,
    bias_stage,
    bias_recv,
    bias_t,
    q_diag,
    k_cols,
    v_aug,
    og_t,
    gated,
    out_cols,
    out_stage,
    out_recv,
    out_rows,
    w_send,
    w_recv,
    pair_sems,
    lr_send,
    lr_recv_sem,
    c_send,
    c_recv_sem,
    bias_sems,
    out_send,
    out_recv_sem,
):
    me = lax.axis_index("dap")
    my_dp = lax.axis_index("dp")
    core = me % 2
    chip_x = (me // 2) % 4
    chip_y = me // 8
    length = length_ref[0]

    def peer(step):
        px = (chip_x + (step // 2) % 4) % 4
        py = (chip_y + step // 8) % 4
        return py * 8 + px * 2 + (core + step % 2) % 2

    def exchange(stage, recv, send_sem, recv_sem):
        def send(step, carry):
            target = peer(step)
            pltpu.make_async_remote_copy(
                src_ref=stage.at[target],
                dst_ref=recv.at[me],
                send_sem=send_sem,
                recv_sem=recv_sem,
                device_id={"dap": target},
                device_id_type=pl.DeviceIdType.MESH,
            ).start()
            return carry

        lax.fori_loop(1, DAP, send, 0)
        pltpu.make_async_copy(stage.at[me], recv.at[me], recv_sem).start()

    def weight_sends(source, dest, index):
        def send(step, carry):
            target = (my_dp + step) % dp_count
            pltpu.make_async_remote_copy(
                src_ref=source,
                dst_ref=dest.at[my_dp],
                send_sem=w_send.at[index],
                recv_sem=w_recv.at[index],
                device_id={"dp": target},
                device_id_type=pl.DeviceIdType.MESH,
            ).start()
            return carry

        lax.fori_loop(1, dp_count, send, 0)
        pltpu.make_async_copy(source, dest.at[my_dp], w_recv.at[index]).start()

    barrier = pltpu.get_barrier_semaphore()

    def greet(step, carry):
        pl.semaphore_signal(
            barrier, inc=1, device_id={"dap": peer(step)}, device_id_type=pl.DeviceIdType.MESH
        )
        return carry

    lax.fori_loop(1, DAP, greet, 0)

    def greet_dp(step, carry):
        pl.semaphore_signal(
            barrier,
            inc=1,
            device_id={"dp": (my_dp + step) % dp_count},
            device_id_type=pl.DeviceIdType.MESH,
        )
        return carry

    lax.fori_loop(1, dp_count, greet_dp, 0)

    def cut_pair(two, carry):
        start = pl.multiple_of(two * 16, 16)
        both = x_ref[0, :, pl.ds(start, 16), :].astype(F32)
        pair_stage[two * 2] = both[:, :8].reshape(64, C).astype(BF16)
        pair_stage[two * 2 + 1] = both[:, 8:].reshape(64, C).astype(BF16)
        return carry

    lax.fori_loop(0, DAP // 2, cut_pair, 0)
    mix_stage[:, 0:128] = tri_gate_ref[...]
    mix_stage[:, 128:256] = tri_output_ref[...]
    mix_stage[:, 256:768] = attn_project_ref[...]
    mix_stage[:, 768:896] = attn_output_ref[...]
    mix_stage[:, 896:1024] = jnp.zeros((mix_stage.shape[0], 128), BF16)
    mix_stage[:, 896:900] = attn_bias_ref[...]

    pl.semaphore_wait(barrier, DAP - 1 + dp_count - 1)

    weight_sends(tri_project_ref, w_tri, 0)
    exchange(pair_stage, pair_recv, pair_sems.at[0], pair_sems.at[1])
    weight_sends(mix_stage, w_mix, 1)
    weight_sends(expand_ref, w_expand, 2)
    weight_sends(reduce_ref, w_reduce, 3)

    def norm_row(row, carry):
        normed_rows[row] = norm_over(x_ref[0, row].astype(F32), 1).astype(BF16)
        return carry

    lax.fori_loop(0, ROWS, norm_row, 0)
    valid_cols = (lax.broadcasted_iota(jnp.int32, (1, TOKENS), 1) < length).astype(F32)

    wait_bytes(w_tri, w_recv.at[0])
    for part in range(4):
        wt_tri[part] = transposed(
            w_tri[:, :, part * C : (part + 1) * C].reshape(C, C)
        )

    for half in range(2):
        span = slice(half * HALF, (half + 1) * HALF)

        def project_row(row, carry):
            normed = normed_rows[row]
            valid_row = (me * ROWS + row < length).astype(F32)
            mask = valid_cols * valid_row
            for side in range(2):
                gate = dot(wt_tri[2 * side, span], normed, NT)
                value = dot(wt_tri[2 * side + 1, span], normed, NT)
                lr_rows_value = sigmoid(gate) * value * mask
                lr_rows[side, 0, pl.ds(row, HALF, stride=ROWS), :] = lr_rows_value[:, :128]
                lr_rows[side, 1, pl.ds(row, HALF, stride=ROWS), :] = lr_rows_value[:, 128:]
            return carry

        lax.fori_loop(0, ROWS, project_row, 0)
        for side in range(2):
            for lanes in range(2):
                lr_stage[half, :, side, :, lanes * 128 : (lanes + 1) * 128] = (
                    lr_rows[side, lanes].astype(BF16).reshape(DAP, 16, 128)
                )
        exchange(lr_stage.at[half], lr_recv.at[half], lr_send.at[half], lr_recv_sem.at[half])

    wait_bytes(w_mix, w_recv.at[1])
    for part in range(8):
        wt_mix[part] = transposed(w_mix[:, :, part * C : (part + 1) * C].reshape(C, C))
    wait_bytes(pair_recv, pair_sems.at[1])
    x_cols[...] = pair_recv[...].astype(F32).reshape(TOKENS * ROWS, C)

    def column_gate(col, carry):
        column = jnp.transpose(x_cols[pl.ds(col, TOKENS, stride=ROWS), :])
        xt[col] = column
        normed = norm_over(column, 0).astype(BF16)
        gate_t[col] = sigmoid(dot(wt_mix[0], normed, NN))
        return carry

    lax.fori_loop(0, ROWS, column_gate, 0)
    v_aug[...] = jnp.ones(v_aug.shape, BF16)
    q_diag[...] = jnp.zeros(q_diag.shape, BF16)

    for half in range(2):
        wait_bytes(lr_recv.at[half], lr_recv_sem.at[half])
        left = lr_recv[half, :, 0].astype(F32)
        right = lr_recv[half, :, 1].astype(F32)
        sums = []
        for channel in range(2):
            rows = slice(channel * ROWS, (channel + 1) * ROWS)
            left_c = left[:, rows].reshape(TOKENS, TOKENS).astype(BF16)
            right_c = right[:, rows].reshape(TOKENS, TOKENS).astype(BF16)
            sums.append(dot(right_c, left_c, NT).reshape(DAP, ROWS, TOKENS))
        c_stage[half] = jnp.concatenate(sums, axis=1).astype(BF16)
        exchange(c_stage.at[half], c_recv.at[half], c_send.at[half], c_recv_sem.at[half])
        if half == 0:
            wait_bytes(w_expand, w_recv.at[2])
            for part in range(8):
                wt_expand[part * C : (part + 1) * C] = transposed(
                    w_expand[:, :, part * C : (part + 1) * C].reshape(C, C)
                )
        else:
            wait_bytes(w_reduce, w_recv.at[3])
            w_reduce_all = w_reduce[...].reshape(FF, C)
            for part in range(FF // C):
                wt_reduce[:, part * C : (part + 1) * C] = transposed(
                    w_reduce_all[part * C : (part + 1) * C]
                )

    wait_bytes(c_recv.at[0], c_recv_sem.at[0])
    wait_bytes(c_recv.at[1], c_recv_sem.at[1])

    def c_sum(step, total):
        return total + c_recv[step // DAP, step % DAP].astype(F32)

    total = lax.fori_loop(0, HALF, c_sum, jnp.zeros((16, TOKENS), F32))
    mean = (total[:8] + total[8:]) * (1.0 / C)
    mean2 = jnp.concatenate([mean, mean], axis=0)

    def c_square(step, total):
        centred = c_recv[step // DAP, step % DAP].astype(F32) - mean2
        return total + centred * centred

    total = lax.fori_loop(0, HALF, c_square, jnp.zeros((16, TOKENS), F32))
    scale = lax.rsqrt((total[:8] + total[8:]) * (1.0 / C) + EPS)
    scale2 = jnp.concatenate([scale, scale], axis=0)

    def c_scale(step, carry):
        value = (c_recv[step // DAP, step % DAP].astype(F32) - mean2) * scale2
        start = pl.multiple_of(step * 16, 16)
        c_normed[0, pl.ds(start, 16), :] = value[:, :128]
        c_normed[1, pl.ds(start, 16), :] = value[:, 128:]
        return carry

    lax.fori_loop(0, HALF, c_scale, 0)

    def column_first(col, carry):
        normed = jnp.concatenate(
            [
                c_normed[0, pl.ds(col, C, stride=ROWS), :],
                c_normed[1, pl.ds(col, C, stride=ROWS), :],
            ],
            axis=1,
        ).astype(BF16)
        first = xt[col] + gate_t[col] * dot(wt_mix[1], normed, NN)
        first_t[col] = first
        first_norm = norm_over(first, 0).astype(BF16)
        first_norm_t[col] = first_norm
        bias = dot(wt_mix[7, 0:16], first_norm, NN)[:8]
        bias_rows[0, pl.ds(col, 8, stride=ROWS), :] = bias[:, :128]
        bias_rows[1, pl.ds(col, 8, stride=ROWS), :] = bias[:, 128:]
        return carry

    lax.fori_loop(0, ROWS, column_first, 0)
    for lanes in range(2):
        bias_stage[:, lanes * 128 : (lanes + 1) * 128] = bias_rows[lanes, 0 : HEADS * ROWS].astype(
            BF16
        )

    def send_bias(step, carry):
        pltpu.make_async_remote_copy(
            src_ref=bias_stage,
            dst_ref=bias_recv.at[me],
            send_sem=bias_sems.at[0],
            recv_sem=bias_sems.at[1],
            device_id={"dap": peer(step)},
            device_id_type=pl.DeviceIdType.MESH,
        ).start()
        return carry

    lax.fori_loop(1, DAP, send_bias, 0)
    pltpu.make_async_copy(bias_stage, bias_recv.at[me], bias_sems.at[1]).start()

    q_scale = LOG2E / HEAD**0.5

    def column_project(col, carry):
        first_norm = first_norm_t[col]
        query = (dot(wt_mix[2], first_norm, NN) * q_scale).astype(BF16)
        value = dot(wt_mix[4], first_norm, NN).astype(BF16)
        og_t[col] = sigmoid(dot(wt_mix[5], first_norm, NN))
        k_cols[col] = transposed(dot(wt_mix[3], first_norm, NN))
        for head in range(HEADS):
            rows = slice(head * HEAD, (head + 1) * HEAD)
            q_diag[col, head, rows, :] = query[rows]
            v_aug[col, head, 0:HEAD, :] = value[rows]
        return carry

    lax.fori_loop(0, ROWS, column_project, 0)

    wait_bytes(bias_recv, bias_sems.at[1])
    masked = jnp.where(
        lax.broadcasted_iota(jnp.int32, (TOKENS, TOKENS), 0) < length, 0.0, -1e9
    )
    for head in range(HEADS):
        rows = slice(head * ROWS, (head + 1) * ROWS)
        bias = bias_recv[:, (head // 2) * 16 : (head // 2) * 16 + 16].astype(F32)
        bias = bias[:, (head % 2) * ROWS : (head % 2 + 1) * ROWS].reshape(TOKENS, TOKENS)
        bias_t[head] = jnp.transpose(bias) * LOG2E + masked

    def column_attend(two, carry):
        for inner in range(2):
            col = two * 2 + inner
            keys = k_cols[col]
            for head in range(HEADS):
                rows = slice(head * HEAD, (head + 1) * HEAD)
                scores = dot(keys, q_diag[col, head], NN) + bias_t[head]
                top = jnp.max(scores, axis=0, keepdims=True)
                soft = jnp.exp2(scores - top).astype(BF16)
                summed = dot(v_aug[col, head], soft, NN)
                attended = summed[0:HEAD] * (1.0 / summed[HEAD : HEAD + 1])
                gated[rows, :] = (attended * og_t[col, rows, :]).astype(BF16)
            second = first_t[col] + dot(wt_mix[6], gated[...], NN)
            second_norm = norm_over(second, 0).astype(BF16)
            hidden = dot(wt_expand[0:FF], second_norm, NN)
            up = dot(wt_expand[FF : 2 * FF], second_norm, NN)
            activated = (hidden * sigmoid(hidden) * up).astype(BF16)
            result = second + dot(wt_reduce[...], activated, NN)
            out_cols[inner] = jnp.transpose(result)
        out_stage[two] = jnp.concatenate(
            [out_cols[0].reshape(DAP, ROWS, C), out_cols[1].reshape(DAP, ROWS, C)], axis=1
        ).astype(BF16)
        exchange(out_stage.at[two], out_recv.at[two], out_send.at[two], out_recv_sem.at[two])
        return carry

    lax.fori_loop(0, ROWS // 2, column_attend, 0)

    for two in range(ROWS // 2):
        wait_bytes(out_recv.at[two], out_recv_sem.at[two])
        out_rows[:, two * 16 : (two + 1) * 16] = out_recv[two].astype(F32)
    flat_rows = out_rows.reshape(TOKENS * ROWS, C)

    def store_row(row, carry):
        out_ref[0, row] = flat_rows[pl.ds(row, TOKENS, stride=ROWS), :].astype(BF16)
        return carry

    lax.fori_loop(0, ROWS, store_row, 0)

    others = pl.ds(0, DAP - 1)
    wait_bytes(w_tri.at[pl.ds(0, dp_count - 1)], w_send.at[0])
    wait_bytes(w_mix.at[pl.ds(0, dp_count - 1)], w_send.at[1])
    wait_bytes(w_expand.at[pl.ds(0, dp_count - 1)], w_send.at[2])
    wait_bytes(w_reduce.at[pl.ds(0, dp_count - 1)], w_send.at[3])
    wait_bytes(pair_stage.at[others], pair_sems.at[0])
    wait_bytes(bias_recv.at[others], bias_sems.at[0])
    for half in range(2):
        wait_bytes(lr_stage.at[half, others], lr_send.at[half])
        wait_bytes(c_stage.at[half, others], c_send.at[half])
    for two in range(ROWS // 2):
        wait_bytes(out_stage.at[two, others], out_send.at[two])


def fused(dp_count, pair_repr, lengths, *weights):
    slice_rows = C // dp_count
    vmem = pl.BlockSpec(memory_space=pltpu.VMEM)
    scratch = [
        pltpu.VMEM((slice_rows, 1024), BF16),
        pltpu.VMEM((dp_count, slice_rows, 512), BF16),
        pltpu.VMEM((dp_count, slice_rows, 1024), BF16),
        pltpu.VMEM((dp_count, slice_rows, 1024), BF16),
        pltpu.VMEM((dp_count, FF // dp_count, C), BF16),
        pltpu.VMEM((4, C, C), BF16),
        pltpu.VMEM((8, C, C), BF16),
        pltpu.VMEM((2 * FF, C), BF16),
        pltpu.VMEM((C, FF), BF16),
        pltpu.VMEM((DAP, 64, C), BF16),
        pltpu.VMEM((DAP, 64, C), BF16),
        pltpu.VMEM((ROWS, TOKENS, C), BF16),
        pltpu.VMEM((2, 2, HALF * ROWS, 128), F32),
        pltpu.VMEM((2, DAP, 2, 16, TOKENS), BF16),
        pltpu.VMEM((2, DAP, 2, 16, TOKENS), BF16),
        pltpu.VMEM((2, DAP, 16, TOKENS), BF16),
        pltpu.VMEM((2, DAP, 16, TOKENS), BF16),
        pltpu.VMEM((2, C * ROWS, 128), F32),
        pltpu.VMEM((TOKENS * ROWS, C), F32),
        pltpu.VMEM((ROWS, C, TOKENS), F32),
        pltpu.VMEM((ROWS, C, TOKENS), F32),
        pltpu.VMEM((ROWS, C, TOKENS), F32),
        pltpu.VMEM((ROWS, C, TOKENS), BF16),
        pltpu.VMEM((2, 64, 128), F32),
        pltpu.VMEM((HEADS * ROWS, TOKENS), BF16),
        pltpu.VMEM((DAP, HEADS * ROWS, TOKENS), BF16),
        pltpu.VMEM((HEADS, TOKENS, TOKENS), F32),
        pltpu.VMEM((ROWS, HEADS, C, TOKENS), BF16),
        pltpu.VMEM((ROWS, TOKENS, C), BF16),
        pltpu.VMEM((ROWS, HEADS, 48, TOKENS), BF16),
        pltpu.VMEM((ROWS, C, TOKENS), F32),
        pltpu.VMEM((C, TOKENS), BF16),
        pltpu.VMEM((2, TOKENS, C), F32),
        pltpu.VMEM((ROWS // 2, DAP, 16, C), BF16),
        pltpu.VMEM((ROWS // 2, DAP, 16, C), BF16),
        pltpu.VMEM((DAP, 64, C), F32),
        pltpu.SemaphoreType.DMA((4,)),
        pltpu.SemaphoreType.DMA((4,)),
        pltpu.SemaphoreType.DMA((2,)),
        pltpu.SemaphoreType.DMA((2,)),
        pltpu.SemaphoreType.DMA((2,)),
        pltpu.SemaphoreType.DMA((2,)),
        pltpu.SemaphoreType.DMA((2,)),
        pltpu.SemaphoreType.DMA((2,)),
        pltpu.SemaphoreType.DMA((ROWS // 2,)),
        pltpu.SemaphoreType.DMA((ROWS // 2,)),
    ]
    return pl.pallas_call(
        functools.partial(body, dp_count),
        out_shape=jax.ShapeDtypeStruct((1, ROWS, TOKENS, C), BF16),
        in_specs=[pl.BlockSpec(memory_space=pltpu.SMEM)] + [vmem] * 9,
        out_specs=vmem,
        scratch_shapes=scratch,
        compiler_params=pltpu.CompilerParams(
            collective_id=0, has_side_effects=True, vmem_limit_bytes=48 * 1024 * 1024
        ),
    )(lengths, pair_repr, *weights)


def solution(mesh):
    dp_count = mesh.shape["dp"]
    placed = (P("dp", "dap", None, None), P("dp")) + (P("dp", None),) * 8
    return jax.shard_map(
        functools.partial(fused, dp_count),
        mesh=mesh,
        in_specs=placed,
        out_specs=P("dp", "dap", None, None),
        check_vma=False,
    )
```

```python
import functools

import jax
import jax.numpy as jnp
from jax import lax
from jax.experimental import pallas as pl
from jax.experimental.pallas import tpu as pltpu
from jax.sharding import PartitionSpec as P

F32 = jnp.float32
BF16 = jnp.bfloat16
NN = (((1,), (0,)), ((), ()))
NT = (((1,), (1,)), ((), ()))
TN = (((0,), (0,)), ((), ()))
LOG2E = 1.4426950408889634
EPS = 1e-05

ROWS = 8
TOKENS = 256
C = 128
HEADS = 4
HEAD = 32
FF = 512
VMEM_LIMIT = 64 * 1024 * 1024 - 65536
DAP = TOKENS // ROWS
HALF = C // 2


OFFSETS = (
    (2, 2), (2, 3), (3, 2), (2, 1), (1, 2), (0, 2), (2, 0), (3, 1),
    (1, 3), (3, 3), (1, 1), (0, 3), (3, 0), (0, 1), (1, 0),
)
MESH = pl.DeviceIdType.MESH


def dot(left, right, dims):
    return lax.dot_general(left, right, dims, preferred_element_type=F32)


def sigmoid(v):
    return 0.5 + 0.5 * jnp.tanh(0.5 * v)


def norm_over(values, axis):
    mean = jnp.mean(values, axis=axis, keepdims=True)
    centred = values - mean
    variance = jnp.mean(centred * centred, axis=axis, keepdims=True)
    return centred * lax.rsqrt(variance + EPS)


def transposed(value):
    return jnp.transpose(value.astype(F32)).astype(BF16)


def wait_bytes(ref, sem):
    pltpu.make_async_copy(ref, ref, sem).wait()


def body(
    dp_count,
    length_ref,
    x_hbm,
    tri_project_ref,
    tri_gate_ref,
    tri_output_ref,
    attn_project_ref,
    attn_bias_ref,
    attn_output_ref,
    expand_ref,
    reduce_ref,
    out_ref,
    x_ref,
    bias_in,
    bias_square,
    mix_stage,
    w_tri,
    w_mix,
    w_expand,
    w_reduce,
    wt_tri,
    wt_mix,
    wt_expand,
    wt_reduce,
    pair_stage,
    pair_recv,
    normed_rows,
    lr_rows,
    lr_stage,
    lr_recv,
    c_stage,
    c_recv,
    c_values,
    c_mean,
    c_scale,
    x_cols,
    xt,
    gate_t,
    first_t,
    first_norm_t,
    bias_rows,
    bias_stage,
    bias_recv,
    bias_t,
    q_diag,
    k_cols,
    v_aug,
    og_t,
    gated,
    out_cols,
    out_stage,
    out_recv,
    out_rows,
    w_send,
    w_recv,
    pair_sems,
    lr_send,
    lr_recv_sem,
    c_send,
    c_recv_sem,
    bias_sems,
    out_send,
    out_recv_sem,
    load_sems,
    ready_sem,
):
    me = lax.axis_index("dap")
    my_dp = lax.axis_index("dp")
    core = me % 2
    chip_x = (me // 2) % 4
    chip_y = me // 8

    sibling = me + 1 - 2 * core

    def chip_of(off_x, off_y):
        return (chip_y + off_y) % 4 * 4 + (chip_x + off_x) % 4

    peers = []
    for off_x, off_y in OFFSETS:
        chip = chip_of(off_x, off_y)
        peers += [chip * 2 + core, chip * 2 + 1 - core]
    peers.append(sibling)

    def exchange(stage, recv, send_sem, recv_sem):
        for target in peers:
            pltpu.make_async_remote_copy(
                src_ref=stage.at[target],
                dst_ref=recv.at[me],
                send_sem=send_sem,
                recv_sem=recv_sem,
                device_id={"dap": target},
                device_id_type=MESH,
            ).start()
        pltpu.make_async_copy(stage.at[me], recv.at[me], recv_sem).start()

    def weight_sends(source, dest, index):
        def send(step, carry):
            target = (my_dp + step) % dp_count
            pltpu.make_async_remote_copy(
                src_ref=source,
                dst_ref=dest.at[my_dp],
                send_sem=w_send.at[index],
                recv_sem=w_recv.at[index],
                device_id={"dp": target},
                device_id_type=MESH,
            ).start()
            return carry

        lax.fori_loop(1, dp_count, send, 0)
        pltpu.make_async_copy(source, dest.at[my_dp], w_recv.at[index]).start()

    load_x = pltpu.make_async_copy(x_hbm, x_ref, load_sems.at[0])
    load_x.start()
    loads = [
        pltpu.make_async_copy(tri_gate_ref, mix_stage.at[:, 0:128], load_sems.at[1]),
        pltpu.make_async_copy(tri_output_ref, mix_stage.at[:, 128:256], load_sems.at[2]),
        pltpu.make_async_copy(attn_project_ref, mix_stage.at[:, 256:768], load_sems.at[3]),
        pltpu.make_async_copy(attn_output_ref, mix_stage.at[:, 768:896], load_sems.at[4]),
        pltpu.make_async_copy(attn_bias_ref, bias_in, load_sems.at[5]),
    ]
    for load in loads:
        load.start()

    barrier = pltpu.get_barrier_semaphore()

    for step in range(1, dp_count):
        pl.semaphore_signal(
            barrier,
            inc=1,
            device_id={"dp": (my_dp + step) % dp_count},
            device_id_type=MESH,
        )
    column_chips = [chip_of(0, off) * 2 + core for off in (2, 1, 3)]
    row_group = []
    for off in (2, 1, 3):
        row_group += [chip_of(off, 0) * 2 + core, chip_of(off, 0) * 2 + 1 - core]
    for target in column_chips + row_group + [sibling]:
        pl.semaphore_signal(barrier, inc=1, device_id={"dap": target}, device_id_type=MESH)

    pl.semaphore_wait(barrier, dp_count - 1 + 10)

    for target in column_chips:
        pl.semaphore_signal(ready_sem, inc=1, device_id={"dap": target}, device_id_type=MESH)
    weight_sends(tri_project_ref, w_tri, 0)
    load_x.wait()

    def cut_pair(two, carry):
        start = pl.multiple_of(two * 16, 16)
        both = x_ref[0, :, pl.ds(start, 16), :].astype(F32)
        pair_stage[two * 2] = both[:, :8].reshape(64, C).astype(BF16)
        pair_stage[two * 2 + 1] = both[:, 8:].reshape(64, C).astype(BF16)
        return carry

    lax.fori_loop(0, DAP // 2, cut_pair, 0, unroll=2)
    pl.semaphore_wait(ready_sem, 3)
    exchange(pair_stage, pair_recv, pair_sems.at[0], pair_sems.at[1])
    for load in loads:
        load.wait()
    slice_rows = mix_stage.shape[0]
    bias_square[...] = jnp.zeros((C, C), F32)
    bias_square[0:HEADS, 0:slice_rows] = bias_in[...].astype(F32)
    mix_stage[:, 896:1024] = jnp.transpose(bias_square[...])[0:slice_rows].astype(BF16)
    weight_sends(mix_stage, w_mix, 1)
    weight_sends(expand_ref, w_expand, 2)
    weight_sends(reduce_ref, w_reduce, 3)

    def norm_row(row, carry):
        normed_rows[row] = norm_over(x_ref[0, row].astype(F32), 1).astype(BF16)
        return carry

    lax.fori_loop(0, ROWS, norm_row, 0, unroll=2)
    length = length_ref[0]
    valid_cols = (lax.broadcasted_iota(jnp.int32, (1, TOKENS), 1) < length).astype(F32)

    wait_bytes(w_tri, w_recv.at[0])
    for part in range(4):
        wt_tri[part] = transposed(
            w_tri[:, :, part * C : (part + 1) * C].reshape(C, C)
        )

    for half in range(2):
        span = slice(half * HALF, (half + 1) * HALF)

        def project_row(row, carry):
            normed = normed_rows[row]
            valid_row = (me * ROWS + row < length).astype(F32)
            mask = valid_cols * valid_row
            for side in range(2):
                gate = dot(wt_tri[2 * side, span], normed, NT)
                value = dot(wt_tri[2 * side + 1, span], normed, NT)
                lr_rows_value = sigmoid(gate) * value * mask
                lr_rows[side, 0, pl.ds(row, HALF, stride=ROWS), :] = lr_rows_value[:, :128]
                lr_rows[side, 1, pl.ds(row, HALF, stride=ROWS), :] = lr_rows_value[:, 128:]
            return carry

        lax.fori_loop(0, ROWS, project_row, 0, unroll=2)
        for side in range(2):
            for lanes in range(2):
                lr_stage[half, :, side, :, lanes * 128 : (lanes + 1) * 128] = (
                    lr_rows[side, lanes].astype(BF16).reshape(DAP, 16, 128)
                )
        exchange(lr_stage.at[half], lr_recv.at[half], lr_send.at[half], lr_recv_sem.at[half])

    wait_bytes(w_mix, w_recv.at[1])
    for part in range(8):
        wt_mix[part] = transposed(w_mix[:, :, part * C : (part + 1) * C].reshape(C, C))
    wait_bytes(pair_recv, pair_sems.at[1])
    x_cols[...] = pair_recv[...].astype(F32).reshape(TOKENS * ROWS, C)

    def column_gate(col, carry):
        column = jnp.transpose(x_cols[pl.ds(col, TOKENS, stride=ROWS), :])
        xt[col] = column
        normed = norm_over(column, 0).astype(BF16)
        gate_t[col] = sigmoid(dot(wt_mix[0], normed, NN))
        return carry

    lax.fori_loop(0, ROWS, column_gate, 0, unroll=2)
    v_aug[...] = jnp.ones(v_aug.shape, BF16)
    q_diag[...] = jnp.zeros(q_diag.shape, BF16)

    for half in range(2):
        wait_bytes(lr_recv.at[half], lr_recv_sem.at[half])
        left = lr_recv[half, :, 0].astype(F32)
        right = lr_recv[half, :, 1].astype(F32)
        sums = []
        for channel in range(2):
            rows = slice(channel * ROWS, (channel + 1) * ROWS)
            left_c = left[:, rows].reshape(TOKENS, TOKENS).astype(BF16)
            right_c = right[:, rows].reshape(TOKENS, TOKENS).astype(BF16)
            sums.append(dot(right_c, left_c, NT).reshape(DAP, ROWS, TOKENS))
        c_stage[half] = jnp.concatenate(sums, axis=1).astype(BF16)
        exchange(c_stage.at[half], c_recv.at[half], c_send.at[half], c_recv_sem.at[half])
        if half == 0:
            wait_bytes(w_expand, w_recv.at[2])
            for part in range(8):
                wt_expand[part * C : (part + 1) * C] = transposed(
                    w_expand[:, :, part * C : (part + 1) * C].reshape(C, C)
                )
        else:
            wait_bytes(w_reduce, w_recv.at[3])
            w_reduce_all = w_reduce[...].reshape(FF, C)
            for part in range(FF // C):
                wt_reduce[:, part * C : (part + 1) * C] = transposed(
                    w_reduce_all[part * C : (part + 1) * C]
                )

    means = []
    squares = []
    for half in range(2):
        wait_bytes(c_recv.at[half], c_recv_sem.at[half])

        def c_sum(step, total):
            for inner in range(4):
                block = step * 4 + inner
                value = c_recv[half, block].astype(F32)
                start = pl.multiple_of(half * 512 + block * 16, 16)
                c_values[0, pl.ds(start, 16), :] = value[:, :128]
                c_values[1, pl.ds(start, 16), :] = value[:, 128:]
                total = total + (value[:8] + value[8:])
            return total

        zero = jnp.zeros((ROWS, TOKENS), F32)
        mean = lax.fori_loop(0, DAP // 4, c_sum, zero) * (1.0 / HALF)

        def c_square(step, total):
            for inner in range(4):
                value = c_recv[half, step * 4 + inner].astype(F32)
                first = value[:8] - mean
                other = value[8:] - mean
                total = total + (first * first + other * other)
            return total

        means.append(mean)
        squares.append(lax.fori_loop(0, DAP // 4, c_square, zero))
    apart = means[0] - means[1]
    variance = (squares[0] + squares[1] + apart * apart * (0.5 * HALF)) * (1.0 / C)
    c_mean[...] = (means[0] + means[1]) * 0.5
    c_scale[...] = lax.rsqrt(variance + EPS)

    def column_first(col, carry):
        values = jnp.concatenate(
            [
                c_values[0, pl.ds(col, C, stride=ROWS), :],
                c_values[1, pl.ds(col, C, stride=ROWS), :],
            ],
            axis=1,
        )
        normed = ((values - c_mean[pl.ds(col, 1), :]) * c_scale[pl.ds(col, 1), :]).astype(BF16)
        first = xt[col] + gate_t[col] * dot(wt_mix[1], normed, NN)
        first_t[col] = first
        first_norm = norm_over(first, 0).astype(BF16)
        first_norm_t[col] = first_norm
        bias = dot(wt_mix[7, 0:16], first_norm, NN)[:8]
        bias_rows[0, pl.ds(col, 8, stride=ROWS), :] = bias[:, :128]
        bias_rows[1, pl.ds(col, 8, stride=ROWS), :] = bias[:, 128:]
        return carry

    lax.fori_loop(0, ROWS, column_first, 0, unroll=4)
    for lanes in range(2):
        bias_stage[:, lanes * 128 : (lanes + 1) * 128] = bias_rows[lanes, 0 : HEADS * ROWS].astype(
            BF16
        )

    for target in peers:
        pltpu.make_async_remote_copy(
            src_ref=bias_stage,
            dst_ref=bias_recv.at[me],
            send_sem=bias_sems.at[0],
            recv_sem=bias_sems.at[1],
            device_id={"dap": target},
            device_id_type=MESH,
        ).start()
    pltpu.make_async_copy(bias_stage, bias_recv.at[me], bias_sems.at[1]).start()

    q_scale = LOG2E / HEAD**0.5

    def column_project(col, carry):
        first_norm = first_norm_t[col]
        query = (dot(wt_mix[2], first_norm, NN) * q_scale).astype(BF16)
        value = dot(wt_mix[4], first_norm, NN).astype(BF16)
        og_t[col] = sigmoid(dot(wt_mix[5], first_norm, NN))
        k_cols[col] = transposed(dot(wt_mix[3], first_norm, NN))
        for head in range(HEADS):
            rows = slice(head * HEAD, (head + 1) * HEAD)
            q_diag[col, head, rows, :] = query[rows]
            v_aug[col, head, 0:HEAD, :] = value[rows]
        return carry

    lax.fori_loop(0, ROWS, column_project, 0, unroll=2)

    wait_bytes(bias_recv, bias_sems.at[1])
    masked = jnp.where(
        lax.broadcasted_iota(jnp.int32, (TOKENS, TOKENS), 0) < length, 0.0, -1e9
    )
    for head in range(HEADS):
        rows = slice(head * ROWS, (head + 1) * ROWS)
        bias = bias_recv[:, (head // 2) * 16 : (head // 2) * 16 + 16].astype(F32)
        bias = bias[:, (head % 2) * ROWS : (head % 2 + 1) * ROWS].reshape(TOKENS, TOKENS)
        bias_t[head] = jnp.transpose(bias) * LOG2E + masked

    def column_attend(two, carry):
        for inner in range(2):
            col = two * 2 + inner
            keys = k_cols[col]
            for head in range(HEADS):
                rows = slice(head * HEAD, (head + 1) * HEAD)
                scores = dot(keys, q_diag[col, head], NN) + bias_t[head]
                top = jnp.max(scores, axis=0, keepdims=True)
                soft = jnp.exp2(scores - top).astype(BF16)
                summed = dot(v_aug[col, head], soft, NN)
                attended = summed[0:HEAD] * (1.0 / summed[HEAD : HEAD + 1])
                gated[rows, :] = (attended * og_t[col, rows, :]).astype(BF16)
            second = first_t[col] + dot(wt_mix[6], gated[...], NN)
            second_norm = norm_over(second, 0).astype(BF16)
            hidden = dot(wt_expand[0:FF], second_norm, NN)
            up = dot(wt_expand[FF : 2 * FF], second_norm, NN)
            activated = (hidden * sigmoid(hidden) * up).astype(BF16)
            result = second + dot(wt_reduce[...], activated, NN)
            out_cols[inner] = jnp.transpose(result)
        out_stage[two] = jnp.concatenate(
            [out_cols[0].reshape(DAP, ROWS, C), out_cols[1].reshape(DAP, ROWS, C)], axis=1
        ).astype(BF16)
        exchange(out_stage.at[two], out_recv.at[two], out_send.at[two], out_recv_sem.at[two])
        return carry

    lax.fori_loop(0, ROWS // 2, column_attend, 0)

    for two in range(ROWS // 2):
        wait_bytes(out_recv.at[two], out_recv_sem.at[two])
        out_rows[:, two * 16 : (two + 1) * 16] = out_recv[two].astype(F32)
    flat_rows = out_rows.reshape(TOKENS * ROWS, C)

    def store_row(row, carry):
        out_ref[0, row] = flat_rows[pl.ds(row, TOKENS, stride=ROWS), :].astype(BF16)
        return carry

    lax.fori_loop(0, ROWS, store_row, 0, unroll=4)

    others = pl.ds(0, DAP - 1)
    wait_bytes(w_tri.at[pl.ds(0, dp_count - 1)], w_send.at[0])
    wait_bytes(w_mix.at[pl.ds(0, dp_count - 1)], w_send.at[1])
    wait_bytes(w_expand.at[pl.ds(0, dp_count - 1)], w_send.at[2])
    wait_bytes(w_reduce.at[pl.ds(0, dp_count - 1)], w_send.at[3])
    wait_bytes(pair_stage.at[others], pair_sems.at[0])
    wait_bytes(bias_recv.at[others], bias_sems.at[0])
    for half in range(2):
        wait_bytes(lr_stage.at[half, others], lr_send.at[half])
        wait_bytes(c_stage.at[half, others], c_send.at[half])
    for two in range(ROWS // 2):
        wait_bytes(out_stage.at[two, others], out_send.at[two])


def fused(dp_count, pair_repr, lengths, *weights):
    slice_rows = C // dp_count
    vmem = pl.BlockSpec(memory_space=pltpu.VMEM)
    anywhere = pl.BlockSpec(memory_space=pltpu.HBM)
    scratch = [
        pltpu.VMEM((1, ROWS, TOKENS, C), BF16),
        pltpu.VMEM((HEADS, slice_rows), BF16),
        pltpu.VMEM((C, C), F32),
        pltpu.VMEM((slice_rows, 1024), BF16),
        pltpu.VMEM((dp_count, slice_rows, 512), BF16),
        pltpu.VMEM((dp_count, slice_rows, 1024), BF16),
        pltpu.VMEM((dp_count, slice_rows, 1024), BF16),
        pltpu.VMEM((dp_count, FF // dp_count, C), BF16),
        pltpu.VMEM((4, C, C), BF16),
        pltpu.VMEM((8, C, C), BF16),
        pltpu.VMEM((2 * FF, C), BF16),
        pltpu.VMEM((C, FF), BF16),
        pltpu.VMEM((DAP, 64, C), BF16),
        pltpu.VMEM((DAP, 64, C), BF16),
        pltpu.VMEM((ROWS, TOKENS, C), BF16),
        pltpu.VMEM((2, 2, HALF * ROWS, 128), F32),
        pltpu.VMEM((2, DAP, 2, 16, TOKENS), BF16),
        pltpu.VMEM((2, DAP, 2, 16, TOKENS), BF16),
        pltpu.VMEM((2, DAP, 16, TOKENS), BF16),
        pltpu.VMEM((2, DAP, 16, TOKENS), BF16),
        pltpu.VMEM((2, C * ROWS, 128), F32),
        pltpu.VMEM((ROWS, TOKENS), F32),
        pltpu.VMEM((ROWS, TOKENS), F32),
        pltpu.VMEM((TOKENS * ROWS, C), F32),
        pltpu.VMEM((ROWS, C, TOKENS), F32),
        pltpu.VMEM((ROWS, C, TOKENS), F32),
        pltpu.VMEM((ROWS, C, TOKENS), F32),
        pltpu.VMEM((ROWS, C, TOKENS), BF16),
        pltpu.VMEM((2, 64, 128), F32),
        pltpu.VMEM((HEADS * ROWS, TOKENS), BF16),
        pltpu.VMEM((DAP, HEADS * ROWS, TOKENS), BF16),
        pltpu.VMEM((HEADS, TOKENS, TOKENS), F32),
        pltpu.VMEM((ROWS, HEADS, C, TOKENS), BF16),
        pltpu.VMEM((ROWS, TOKENS, C), BF16),
        pltpu.VMEM((ROWS, HEADS, 48, TOKENS), BF16),
        pltpu.VMEM((ROWS, C, TOKENS), F32),
        pltpu.VMEM((C, TOKENS), BF16),
        pltpu.VMEM((2, TOKENS, C), F32),
        pltpu.VMEM((ROWS // 2, DAP, 16, C), BF16),
        pltpu.VMEM((ROWS // 2, DAP, 16, C), BF16),
        pltpu.VMEM((DAP, 64, C), F32),
        pltpu.SemaphoreType.DMA((4,)),
        pltpu.SemaphoreType.DMA((4,)),
        pltpu.SemaphoreType.DMA((2,)),
        pltpu.SemaphoreType.DMA((2,)),
        pltpu.SemaphoreType.DMA((2,)),
        pltpu.SemaphoreType.DMA((2,)),
        pltpu.SemaphoreType.DMA((2,)),
        pltpu.SemaphoreType.DMA((2,)),
        pltpu.SemaphoreType.DMA((ROWS // 2,)),
        pltpu.SemaphoreType.DMA((ROWS // 2,)),
        pltpu.SemaphoreType.DMA((6,)),
        pltpu.SemaphoreType.REGULAR,
    ]
    return pl.pallas_call(
        functools.partial(body, dp_count),
        out_shape=jax.ShapeDtypeStruct((1, ROWS, TOKENS, C), BF16),
        in_specs=[pl.BlockSpec(memory_space=pltpu.SMEM)] + [anywhere] * 9,
        out_specs=vmem,
        scratch_shapes=scratch,
        compiler_params=pltpu.CompilerParams(
            collective_id=0, has_side_effects=True, vmem_limit_bytes=VMEM_LIMIT
        ),
    )(lengths, pair_repr, *weights[:4], jnp.transpose(weights[4]), *weights[5:])


def solution(mesh):
    dp_count = mesh.shape["dp"]
    placed = (P("dp", "dap", None, None), P("dp")) + (P("dp", None),) * 8
    return jax.shard_map(
        functools.partial(fused, dp_count),
        mesh=mesh,
        in_specs=placed,
        out_specs=P("dp", "dap", None, None),
        check_vma=False,
    )
```

```python
import functools

import jax
import jax.numpy as jnp
from jax import lax
from jax.experimental import pallas as pl
from jax.experimental.pallas import tpu as pltpu
from jax.sharding import PartitionSpec as P

F32 = jnp.float32
BF16 = jnp.bfloat16
NN = (((1,), (0,)), ((), ()))
NT = (((1,), (1,)), ((), ()))
TN = (((0,), (0,)), ((), ()))
LOG2E = 1.4426950408889634
EPS = 1e-05

ROWS = 8
TOKENS = 256
C = 128
HEADS = 4
HEAD = 32
FF = 512
VMEM_LIMIT = 64 * 1024 * 1024 - 65536
DAP = TOKENS // ROWS
PARTS = 4
PART = C // PARTS
GROUP = ROWS // 2


OFFSETS = (
    (2, 2), (2, 3), (3, 2), (2, 1), (1, 2), (0, 2), (2, 0), (3, 1),
    (1, 3), (3, 3), (1, 1), (0, 3), (3, 0), (0, 1), (1, 0),
)
MESH = pl.DeviceIdType.MESH


def dot(left, right, dims):
    return lax.dot_general(left, right, dims, preferred_element_type=F32)


def sigmoid(v):
    return 0.5 + 0.5 * jnp.tanh(0.5 * v)


def norm_over(values, axis):
    mean = jnp.mean(values, axis=axis, keepdims=True)
    centred = values - mean
    variance = jnp.mean(centred * centred, axis=axis, keepdims=True)
    return centred * lax.rsqrt(variance + EPS)


def transposed(value):
    return jnp.transpose(value.astype(F32)).astype(BF16)


def wait_bytes(ref, sem):
    pltpu.make_async_copy(ref, ref, sem).wait()


def body(
    dp_count,
    length_ref,
    x_hbm,
    tri_project_ref,
    tri_gate_ref,
    tri_output_ref,
    attn_project_ref,
    attn_bias_ref,
    attn_output_ref,
    expand_ref,
    reduce_ref,
    out_ref,
    x_ref,
    bias_in,
    bias_square,
    tri_in,
    tri_stage,
    mix_stage,
    w_tri,
    w_mix,
    w_expand,
    w_reduce,
    wt_tri,
    wt_mix,
    wt_expand,
    wt_reduce,
    pair_stage,
    pair_recv,
    normed_rows,
    lr_rows,
    lr_stage,
    lr_recv,
    c_stage,
    c_recv,
    c_values,
    c_mean,
    c_scale,
    x_cols,
    xt,
    gate_t,
    first_t,
    first_norm_t,
    bias_rows,
    bias_stage,
    bias_recv,
    bias_t,
    q_diag,
    k_cols,
    v_aug,
    og_t,
    scores_ref,
    out_stage,
    out_recv,
    out_rows,
    w_send,
    w_recv,
    relay_send,
    relay_recv,
    pair_sems,
    lr_send,
    lr_recv_sem,
    c_send,
    c_recv_sem,
    bias_send,
    bias_recv_sem,
    bias_relay_send,
    bias_relay_recv,
    out_send,
    out_recv_sem,
    load_sems,
    ready_sem,
):
    me = lax.axis_index("dap")
    my_dp = lax.axis_index("dp")
    core = me % 2
    my_chip = me // 2
    chip_x = (me // 2) % 4
    chip_y = me // 8

    sibling = me + 1 - 2 * core

    def chip_of(off_x, off_y):
        return (chip_y + off_y) % 4 * 4 + (chip_x + off_x) % 4

    peers = []
    same_core = []
    unheard = []
    for off_x, off_y in OFFSETS:
        chip = chip_of(off_x, off_y)
        both = [chip * 2 + core, chip * 2 + 1 - core]
        peers += both
        same_core += both[:1]
        if off_y != 0:
            unheard += both if off_x != 0 else both[1:]
    peers.append(sibling)

    def send_blocks(targets, stage, recv, send_sem, recv_sem):
        for target in targets:
            pltpu.make_async_remote_copy(
                src_ref=stage.at[target],
                dst_ref=recv.at[me],
                send_sem=send_sem,
                recv_sem=recv_sem,
                device_id={"dap": target},
                device_id_type=MESH,
            ).start()

    pending = []

    def exchange(stage, recv, send_sem, recv_sem):
        send_blocks(peers, stage, recv, send_sem, recv_sem)
        pltpu.make_async_copy(stage.at[me], recv.at[me], recv_sem).start()
        pending.append((stage.at[pl.ds(0, DAP - 1)], send_sem))

    def weight_sends(source, dest, index):
        def send(step, carry):
            target = (my_dp + step) % dp_count
            pltpu.make_async_remote_copy(
                src_ref=source,
                dst_ref=dest.at[my_dp],
                send_sem=w_send.at[index],
                recv_sem=w_recv.at[index],
                device_id={"dp": target},
                device_id_type=MESH,
            ).start()
            return carry

        lax.fori_loop(1, dp_count, send, 0)
        pltpu.make_async_copy(source, dest.at[my_dp], w_recv.at[index]).start()
        pending.append((dest.at[pl.ds(0, dp_count - 1)], w_send.at[index]))

    load_x = pltpu.make_async_copy(x_hbm, x_ref, load_sems.at[0])
    load_x.start()
    load_tri = pltpu.make_async_copy(tri_project_ref, tri_in, load_sems.at[7])
    load_tri.start()
    loads = [
        pltpu.make_async_copy(tri_gate_ref, mix_stage.at[0, :, 0:128], load_sems.at[1]),
        pltpu.make_async_copy(tri_output_ref, mix_stage.at[0, :, 128:256], load_sems.at[2]),
        pltpu.make_async_copy(
            attn_project_ref.at[:, 0:256], mix_stage.at[0, :, 256:512], load_sems.at[3]
        ),
        pltpu.make_async_copy(
            attn_project_ref.at[:, 256:512], mix_stage.at[1, :, 0:256], load_sems.at[6]
        ),
        pltpu.make_async_copy(attn_output_ref, mix_stage.at[1, :, 256:384], load_sems.at[4]),
        pltpu.make_async_copy(attn_bias_ref, bias_in, load_sems.at[5]),
    ]
    for load in loads:
        load.start()

    def relay(weights, index):
        wait_bytes(weights.at[0], w_recv.at[index])
        pltpu.make_async_remote_copy(
            src_ref=weights.at[core],
            dst_ref=weights.at[core],
            send_sem=relay_send.at[index],
            recv_sem=relay_recv.at[index],
            device_id={"dap": sibling},
            device_id_type=MESH,
        ).start()
        pending.append((weights.at[0], relay_send.at[index]))

    barrier = pltpu.get_barrier_semaphore()

    for step in range(1, dp_count):
        pl.semaphore_signal(
            barrier,
            inc=1,
            device_id={"dp": (my_dp + step) % dp_count},
            device_id_type=MESH,
        )
    column_chips = [chip_of(0, off) * 2 + core for off in (2, 1, 3)]
    row_group = []
    for off in (2, 1, 3):
        row_group += [chip_of(off, 0) * 2 + core, chip_of(off, 0) * 2 + 1 - core]
    for target in column_chips + row_group + [sibling]:
        pl.semaphore_signal(barrier, inc=1, device_id={"dap": target}, device_id_type=MESH)

    load_tri.wait()
    tri_whole = tri_in[...].astype(F32)
    for quarter in range(PARTS):
        tri_stage[quarter] = jnp.concatenate(
            [
                tri_whole[:, part * C + quarter * PART : part * C + (quarter + 1) * PART]
                for part in range(4)
            ],
            axis=1,
        ).astype(BF16)

    load_x.wait()

    def cut_pair(two, carry):
        start = pl.multiple_of(two * 16, 16)
        both = x_ref[0, :, pl.ds(start, 16), :].astype(F32)
        pair_stage[two * 2] = both[:, :8].reshape(64, C).astype(BF16)
        pair_stage[two * 2 + 1] = both[:, 8:].reshape(64, C).astype(BF16)
        return carry

    lax.fori_loop(0, DAP // 2, cut_pair, 0, unroll=2)

    def norm_row(row, carry):
        normed_rows[row] = norm_over(x_ref[0, row].astype(F32), 1).astype(BF16)
        return carry

    lax.fori_loop(0, ROWS, norm_row, 0, unroll=2)
    pl.semaphore_wait(barrier, dp_count - 1 + 10)

    for target in column_chips:
        pl.semaphore_signal(ready_sem, inc=1, device_id={"dap": target}, device_id_type=MESH)
    weight_sends(tri_stage.at[0], w_tri.at[0], 4)
    heard = row_group + column_chips + [sibling]
    send_blocks(heard, pair_stage, pair_recv, pair_sems.at[0], pair_sems.at[1])

    for quarter in range(1, PARTS):
        weight_sends(tri_stage.at[quarter], w_tri.at[quarter], 4 + quarter)
    pl.semaphore_wait(ready_sem, 3)
    send_blocks(unheard, pair_stage, pair_recv, pair_sems.at[0], pair_sems.at[1])
    pltpu.make_async_copy(pair_stage.at[me], pair_recv.at[me], pair_sems.at[1]).start()
    pending.append((pair_stage.at[pl.ds(0, DAP - 1)], pair_sems.at[0]))

    length = length_ref[0]
    valid_cols = (lax.broadcasted_iota(jnp.int32, (1, TOKENS), 1) < length).astype(F32)

    for quarter in range(PARTS):
        wait_bytes(w_tri.at[quarter], w_recv.at[4 + quarter])
        wt_tri[quarter] = transposed(w_tri[quarter].reshape(C, C))

        def project_row(row, carry):
            valid_row = (me * ROWS + row < length).astype(F32)
            mask = valid_cols * valid_row
            projected = dot(wt_tri[quarter], normed_rows[row], NT)
            for side in range(2):
                gate = projected[2 * side * PART : (2 * side + 1) * PART]
                value = projected[(2 * side + 1) * PART : (2 * side + 2) * PART]
                kept = sigmoid(gate) * value * mask
                lr_rows[side, 0, pl.ds(row, PART, stride=ROWS), :] = kept[:, :128]
                lr_rows[side, 1, pl.ds(row, PART, stride=ROWS), :] = kept[:, 128:]
            return carry

        lax.fori_loop(0, ROWS, project_row, 0, unroll=4)
        for lanes in range(2):
            lr_stage[quarter, :, :, lanes * 128 : (lanes + 1) * 128] = jnp.concatenate(
                [lr_rows[side, lanes].reshape(DAP, ROWS, 128) for side in range(2)], axis=1
            ).astype(BF16)
        exchange(
            lr_stage.at[quarter],
            lr_recv.at[quarter],
            lr_send.at[quarter],
            lr_recv_sem.at[quarter],
        )
        if quarter > 0:
            continue

        for load in loads:
            load.wait()
        slice_rows = mix_stage.shape[1]
        bias_square[...] = jnp.zeros((C, C), F32)
        bias_square[0:HEADS, 0:slice_rows] = bias_in[...].astype(F32)
        mix_stage[1, :, 384:512] = jnp.transpose(bias_square[...])[0:slice_rows].astype(BF16)
        lanes = pl.ds(pl.multiple_of(core * FF, FF), FF)
        rows_sent = reduce_ref.shape[0] // 2
        rows = pl.ds(pl.multiple_of(core * rows_sent, rows_sent), rows_sent)
        weight_sends(mix_stage.at[core], w_mix.at[core], 1)
        weight_sends(expand_ref.at[:, lanes], w_expand.at[core], 2)
        weight_sends(reduce_ref.at[rows, :], w_reduce.at[core], 3)

    relay(w_mix, 1)
    wait_bytes(pair_recv, pair_sems.at[1])
    x_cols[...] = pair_recv[...].astype(F32).reshape(TOKENS * ROWS, C)

    wait_bytes(w_mix.at[0], relay_recv.at[1])
    for part in range(8):
        wt_mix[part] = transposed(
            w_mix[part // 4, :, :, (part % 4) * C : (part % 4 + 1) * C].reshape(C, C)
        )

    def column_gate(col, carry):
        column = jnp.transpose(x_cols[pl.ds(col, TOKENS, stride=ROWS), :])
        xt[col] = column
        normed = norm_over(column, 0).astype(BF16)
        gate_t[col] = sigmoid(dot(wt_mix[0], normed, NN))
        return carry

    lax.fori_loop(0, ROWS, column_gate, 0, unroll=2)
    v_aug[...] = jnp.ones(v_aug.shape, BF16)
    q_diag[...] = jnp.zeros(q_diag.shape, BF16)

    for quarter in range(PARTS):
        wait_bytes(lr_recv.at[quarter], lr_recv_sem.at[quarter])
        both = lr_recv[quarter].astype(F32)
        left = both[:, :ROWS].reshape(TOKENS, TOKENS).astype(BF16)
        right = both[:, ROWS:].reshape(TOKENS, TOKENS).astype(BF16)
        total = dot(right, left, NT)
        c_stage[quarter] = jnp.concatenate(
            [
                total[:, :128].reshape(DAP, ROWS, 128),
                total[:, 128:].reshape(DAP, ROWS, 128),
            ],
            axis=1,
        ).astype(BF16)
        exchange(
            c_stage.at[quarter],
            c_recv.at[quarter],
            c_send.at[quarter],
            c_recv_sem.at[quarter],
        )
        if quarter == 1:
            relay(w_expand, 2)
        if quarter == 2:
            relay(w_reduce, 3)

    wait_bytes(w_expand.at[0], relay_recv.at[2])
    for part in range(8):
        wt_expand[part * C : (part + 1) * C] = transposed(
            w_expand[part // 4, :, :, (part % 4) * C : (part % 4 + 1) * C].reshape(C, C)
        )
    wait_bytes(w_reduce.at[0], relay_recv.at[3])
    blocks = [(half, index) for index in range(dp_count) for half in range(2)]
    for part in range(FF // C):
        own = blocks[part * len(blocks) * C // FF : (part + 1) * len(blocks) * C // FF]
        wt_reduce[:, part * C : (part + 1) * C] = transposed(
            jnp.concatenate([w_reduce[half, index] for half, index in own], axis=0)
        )

    means = []
    squares = []
    zero = jnp.zeros((16, 128), F32)
    for quarter in range(PARTS):
        wait_bytes(c_recv.at[quarter], c_recv_sem.at[quarter])

        def c_sum(step, total):
            for inner in range(4):
                block = step * 4 + inner
                value = c_recv[quarter, block].astype(F32)
                start = pl.multiple_of((quarter * PART + block) * ROWS, ROWS)
                c_values[0, pl.ds(start, ROWS), :] = value[:ROWS]
                c_values[1, pl.ds(start, ROWS), :] = value[ROWS:]
                total = total + value
            return total

        mean = lax.fori_loop(0, PART // 4, c_sum, zero) * (1.0 / PART)

        def c_square(step, total):
            for inner in range(4):
                apart = c_recv[quarter, step * 4 + inner].astype(F32) - mean
                total = total + apart * apart
            return total

        means.append(mean)
        squares.append(lax.fori_loop(0, PART // 4, c_square, zero))
    mean = sum(means) * (1.0 / PARTS)
    variance = sum(
        square + (own - mean) * (own - mean) * PART for square, own in zip(squares, means)
    ) * (1.0 / C)
    scale = lax.rsqrt(variance + EPS)
    c_mean[...] = jnp.concatenate([mean[:ROWS], mean[ROWS:]], axis=1)
    c_scale[...] = jnp.concatenate([scale[:ROWS], scale[ROWS:]], axis=1)

    def column_first(col, carry):
        values = jnp.concatenate(
            [
                c_values[0, pl.ds(col, C, stride=ROWS), :],
                c_values[1, pl.ds(col, C, stride=ROWS), :],
            ],
            axis=1,
        )
        normed = ((values - c_mean[pl.ds(col, 1), :]) * c_scale[pl.ds(col, 1), :]).astype(BF16)
        first = xt[col] + gate_t[col] * dot(wt_mix[1], normed, NN)
        first_t[col] = first
        first_norm = norm_over(first, 0).astype(BF16)
        first_norm_t[col] = first_norm
        bias = dot(wt_mix[7, 0:16], first_norm, NN)[:8]
        slot = col // GROUP
        inner = col - slot * GROUP
        bias_rows[slot, 0, pl.ds(inner, 8, stride=GROUP), :] = bias[:, :128]
        bias_rows[slot, 1, pl.ds(inner, 8, stride=GROUP), :] = bias[:, 128:]
        return carry

    for half in range(2):
        lax.fori_loop(half * GROUP, (half + 1) * GROUP, column_first, 0, unroll=4)
        for lanes in range(2):
            bias_stage[half, :, lanes * 128 : (lanes + 1) * 128] = bias_rows[
                half, lanes, 0 : HEADS * GROUP
            ].astype(BF16)
        for target in same_core:
            pltpu.make_async_remote_copy(
                src_ref=bias_stage.at[half],
                dst_ref=bias_recv.at[half, core, my_chip],
                send_sem=bias_send.at[half],
                recv_sem=bias_recv_sem.at[half],
                device_id={"dap": target},
                device_id_type=MESH,
            ).start()
        pltpu.make_async_copy(
            bias_stage.at[half], bias_recv.at[half, core, my_chip], bias_recv_sem.at[half]
        ).start()
        pending.append((bias_recv.at[half, 0, pl.ds(0, DAP // 2 - 1)], bias_send.at[half]))

    def relay_bias(half):
        wait_bytes(bias_recv.at[half, 0], bias_recv_sem.at[half])
        pltpu.make_async_remote_copy(
            src_ref=bias_recv.at[half, core],
            dst_ref=bias_recv.at[half, core],
            send_sem=bias_relay_send.at[half],
            recv_sem=bias_relay_recv.at[half],
            device_id={"dap": sibling},
            device_id_type=MESH,
        ).start()
        pending.append((bias_recv.at[half, 0], bias_relay_send.at[half]))

    q_scale = LOG2E / HEAD**0.5

    def column_project(col, carry):
        first_norm = first_norm_t[col]
        query = (dot(wt_mix[2], first_norm, NN) * q_scale).astype(BF16)
        value = dot(wt_mix[4], first_norm, NN).astype(BF16)
        og_t[col] = sigmoid(dot(wt_mix[5], first_norm, NN))
        k_cols[col] = transposed(dot(wt_mix[3], first_norm, NN))
        for head in range(HEADS):
            rows = slice(head * HEAD, (head + 1) * HEAD)
            q_diag[col, rows, head * TOKENS : (head + 1) * TOKENS] = query[rows]
            v_aug[col, head, 0:HEAD, :] = value[rows]
        return carry

    lax.fori_loop(0, ROWS, column_project, 0, unroll=2)

    relay_bias(0)
    def column_scores(col, carry):
        for head in range(HEADS):
            lanes = slice(head * TOKENS, (head + 1) * TOKENS)
            scores_ref[col, :, lanes] = dot(k_cols[col], q_diag[col, :, lanes], NN)
        return carry

    lax.fori_loop(0, ROWS, column_scores, 0)
    relay_bias(1)
    for half in range(2):
        wait_bytes(bias_recv.at[half, 0], bias_relay_recv.at[half])
    masked = jnp.where(
        lax.broadcasted_iota(jnp.int32, (TOKENS, TOKENS), 0) < length, 0.0, -1e9
    )
    for pair in range(HEADS // 2):
        tiles = []
        for half in range(2):
            by_core = bias_recv[half].astype(F32)[:, :, pair * 8 : pair * 8 + 8]
            by_chip = [by_core[own, chip] for chip in range(DAP // 2) for own in range(2)]
            tiles.append(jnp.stack(by_chip, axis=0))
        low = lax.broadcasted_iota(jnp.int32, (DAP, 8, TOKENS), 1) < GROUP
        swapped = [pltpu.roll(tile, GROUP, 1) for tile in tiles]
        heads = (
            jnp.where(low, tiles[0], swapped[1]),
            jnp.where(low, swapped[0], tiles[1]),
        )
        for inner in range(2):
            turned = jnp.transpose(heads[inner].reshape(TOKENS, TOKENS))
            head = pair * 2 + inner
            bias_t[:, head * TOKENS : (head + 1) * TOKENS] = turned * LOG2E + masked

    def column_attend(two, carry):
        cols = [two * 2, two * 2 + 1]
        seconds = []
        for col in cols:
            scores = [
                scores_ref[col, :, head * TOKENS : (head + 1) * TOKENS]
                + bias_t[:, head * TOKENS : (head + 1) * TOKENS]
                for head in range(HEADS)
            ]
            softs = [
                jnp.exp2(score - jnp.max(score, axis=0, keepdims=True)).astype(BF16)
                for score in scores
            ]
            sums = [dot(v_aug[col, head], softs[head], NN) for head in range(HEADS)]
            attended = jnp.concatenate(
                [total[0:HEAD] * (1.0 / total[HEAD : HEAD + 1]) for total in sums], axis=0
            )
            gated = (attended * og_t[col]).astype(BF16)
            seconds.append(first_t[col] + dot(wt_mix[6], gated, NN))
        norms = [norm_over(second, 0).astype(BF16) for second in seconds]
        hiddens = [dot(wt_expand[0:FF], norm, NN) for norm in norms]
        ups = [dot(wt_expand[FF : 2 * FF], norm, NN) for norm in norms]
        activated = [
            (hidden * sigmoid(hidden) * up).astype(BF16) for hidden, up in zip(hiddens, ups)
        ]
        results = [
            jnp.transpose(second + dot(wt_reduce[...], act, NN)).reshape(DAP, ROWS, C)
            for second, act in zip(seconds, activated)
        ]
        out_stage[two] = jnp.concatenate(results, axis=1).astype(BF16)
        exchange(out_stage.at[two], out_recv.at[two], out_send.at[two], out_recv_sem.at[two])
        pending.pop()
        return carry

    lax.fori_loop(0, ROWS // 2, column_attend, 0, unroll=2)

    for two in range(ROWS // 2):
        wait_bytes(out_recv.at[two], out_recv_sem.at[two])
        out_rows[:, two * 16 : (two + 1) * 16] = out_recv[two].astype(F32)
    flat_rows = out_rows.reshape(TOKENS * ROWS, C)

    def store_row(row, carry):
        out_ref[0, row] = flat_rows[pl.ds(row, TOKENS, stride=ROWS), :].astype(BF16)
        return carry

    lax.fori_loop(0, ROWS, store_row, 0, unroll=4)

    for two in range(ROWS // 2):
        wait_bytes(out_stage.at[two, pl.ds(0, DAP - 1)], out_send.at[two])
    for ref, sem in pending:
        wait_bytes(ref, sem)


def fused(dp_count, pair_repr, lengths, *weights):
    slice_rows = C // dp_count
    vmem = pl.BlockSpec(memory_space=pltpu.VMEM)
    anywhere = pl.BlockSpec(memory_space=pltpu.HBM)
    scratch = [
        pltpu.VMEM((1, ROWS, TOKENS, C), BF16),
        pltpu.VMEM((HEADS, slice_rows), BF16),
        pltpu.VMEM((C, C), F32),
        pltpu.VMEM((slice_rows, 4 * C), BF16),
        pltpu.VMEM((PARTS, slice_rows, C), BF16),
        pltpu.VMEM((2, slice_rows, FF), BF16),
        pltpu.VMEM((PARTS, dp_count, slice_rows, C), BF16),
        pltpu.VMEM((2, dp_count, slice_rows, FF), BF16),
        pltpu.VMEM((2, dp_count, slice_rows, FF), BF16),
        pltpu.VMEM((2, dp_count, FF // dp_count // 2, C), BF16),
        pltpu.VMEM((PARTS, C, C), BF16),
        pltpu.VMEM((8, C, C), BF16),
        pltpu.VMEM((2 * FF, C), BF16),
        pltpu.VMEM((C, FF), BF16),
        pltpu.VMEM((DAP, 64, C), BF16),
        pltpu.VMEM((DAP, 64, C), BF16),
        pltpu.VMEM((ROWS, TOKENS, C), BF16),
        pltpu.VMEM((2, 2, PART * ROWS, 128), F32),
        pltpu.VMEM((PARTS, DAP, 16, TOKENS), BF16),
        pltpu.VMEM((PARTS, DAP, 16, TOKENS), BF16),
        pltpu.VMEM((PARTS, DAP, 16, 128), BF16),
        pltpu.VMEM((PARTS, DAP, 16, 128), BF16),
        pltpu.VMEM((2, C * ROWS, 128), F32),
        pltpu.VMEM((ROWS, TOKENS), F32),
        pltpu.VMEM((ROWS, TOKENS), F32),
        pltpu.VMEM((TOKENS * ROWS, C), F32),
        pltpu.VMEM((ROWS, C, TOKENS), F32),
        pltpu.VMEM((ROWS, C, TOKENS), F32),
        pltpu.VMEM((ROWS, C, TOKENS), F32),
        pltpu.VMEM((ROWS, C, TOKENS), BF16),
        pltpu.VMEM((2, 2, 8 * GROUP, 128), F32),
        pltpu.VMEM((2, HEADS * GROUP, TOKENS), BF16),
        pltpu.VMEM((2, 2, DAP // 2, HEADS * GROUP, TOKENS), BF16),
        pltpu.VMEM((TOKENS, HEADS * TOKENS), F32),
        pltpu.VMEM((ROWS, C, HEADS * TOKENS), BF16),
        pltpu.VMEM((ROWS, TOKENS, C), BF16),
        pltpu.VMEM((ROWS, HEADS, 48, TOKENS), BF16),
        pltpu.VMEM((ROWS, C, TOKENS), F32),
        pltpu.VMEM((ROWS, TOKENS, HEADS * TOKENS), F32),
        pltpu.VMEM((ROWS // 2, DAP, 16, C), BF16),
        pltpu.VMEM((ROWS // 2, DAP, 16, C), BF16),
        pltpu.VMEM((DAP, 64, C), F32),
        pltpu.SemaphoreType.DMA((4 + PARTS,)),
        pltpu.SemaphoreType.DMA((4 + PARTS,)),
        pltpu.SemaphoreType.DMA((4,)),
        pltpu.SemaphoreType.DMA((4,)),
        pltpu.SemaphoreType.DMA((2,)),
        pltpu.SemaphoreType.DMA((PARTS,)),
        pltpu.SemaphoreType.DMA((PARTS,)),
        pltpu.SemaphoreType.DMA((PARTS,)),
        pltpu.SemaphoreType.DMA((PARTS,)),
        pltpu.SemaphoreType.DMA((2,)),
        pltpu.SemaphoreType.DMA((2,)),
        pltpu.SemaphoreType.DMA((2,)),
        pltpu.SemaphoreType.DMA((2,)),
        pltpu.SemaphoreType.DMA((ROWS // 2,)),
        pltpu.SemaphoreType.DMA((ROWS // 2,)),
        pltpu.SemaphoreType.DMA((8,)),
        pltpu.SemaphoreType.REGULAR,
    ]
    return pl.pallas_call(
        functools.partial(body, dp_count),
        out_shape=jax.ShapeDtypeStruct((1, ROWS, TOKENS, C), BF16),
        in_specs=[pl.BlockSpec(memory_space=pltpu.SMEM)] + [anywhere] * 9,
        out_specs=vmem,
        scratch_shapes=scratch,
        compiler_params=pltpu.CompilerParams(
            collective_id=0, has_side_effects=True, vmem_limit_bytes=VMEM_LIMIT
        ),
    )(lengths, pair_repr, *weights[:4], jnp.transpose(weights[4]), *weights[5:])


def solution(mesh):
    dp_count = mesh.shape["dp"]
    placed = (P("dp", "dap", None, None), P("dp")) + (P("dp", None),) * 8
    return jax.shard_map(
        functools.partial(fused, dp_count),
        mesh=mesh,
        in_specs=placed,
        out_specs=P("dp", "dap", None, None),
        check_vma=False,
    )
```

```python
import functools

import jax
import jax.numpy as jnp
from jax import lax
from jax.experimental import pallas as pl
from jax.experimental.pallas import tpu as pltpu
from jax.sharding import PartitionSpec as P

F32 = jnp.float32
BF16 = jnp.bfloat16
NN = (((1,), (0,)), ((), ()))
NT = (((1,), (1,)), ((), ()))
TN = (((0,), (0,)), ((), ()))
LOG2E = 1.4426950408889634
EPS = 1e-05

ROWS = 8
TOKENS = 256
C = 128
HEADS = 4
HEAD = 32
FF = 512
VMEM_LIMIT = 64 * 1024 * 1024 - 65536
DAP = TOKENS // ROWS
PARTS = 4
PART = C // PARTS
GROUP = ROWS // 2


OFFSETS = (
    (2, 2), (2, 3), (3, 2), (2, 1), (1, 2), (0, 2), (2, 0), (3, 1),
    (1, 3), (3, 3), (1, 1), (0, 3), (3, 0), (0, 1), (1, 0),
)
MESH = pl.DeviceIdType.MESH


def dot(left, right, dims):
    return lax.dot_general(left, right, dims, preferred_element_type=F32)


def sigmoid(v):
    return 0.5 + 0.5 * jnp.tanh(0.5 * v)


def norm_over(values, axis):
    mean = jnp.mean(values, axis=axis, keepdims=True)
    centred = values - mean
    variance = jnp.mean(centred * centred, axis=axis, keepdims=True)
    return centred * lax.rsqrt(variance + EPS)


def transposed(value):
    return jnp.transpose(value.astype(F32)).astype(BF16)


def wait_bytes(ref, sem):
    pltpu.make_async_copy(ref, ref, sem).wait()


def body(
    dp_count,
    length_ref,
    x_hbm,
    tri_project_ref,
    tri_gate_ref,
    tri_output_ref,
    attn_project_ref,
    attn_bias_ref,
    attn_output_ref,
    expand_ref,
    reduce_ref,
    out_recv,
    x_ref,
    bias_in,
    bias_square,
    tri_in,
    tri_stage,
    mix_stage,
    w_tri,
    w_mix,
    w_expand,
    w_reduce,
    wt_tri,
    wt_mix,
    wt_expand,
    wt_reduce,
    pair_stage,
    pair_recv,
    normed_rows,
    lr_rows,
    lr_stage,
    lr_recv,
    c_stage,
    c_recv,
    c_values,
    c_mean,
    c_scale,
    x_cols,
    xt,
    gate_t,
    first_t,
    first_norm_t,
    bias_rows,
    bias_stage,
    bias_recv,
    bias_t,
    q_diag,
    k_cols,
    v_aug,
    og_t,
    scores_ref,
    second_t,
    out_stage,
    w_send,
    w_recv,
    relay_send,
    relay_recv,
    pair_sems,
    lr_send,
    lr_recv_sem,
    c_send,
    c_recv_sem,
    bias_send,
    bias_recv_sem,
    bias_relay_send,
    bias_relay_recv,
    out_send,
    out_recv_sem,
    load_sems,
    ready_sem,
):
    me = lax.axis_index("dap")
    my_dp = lax.axis_index("dp")
    core = me % 2
    my_chip = me // 2
    chip_x = (me // 2) % 4
    chip_y = me // 8

    sibling = me + 1 - 2 * core

    def chip_of(off_x, off_y):
        return (chip_y + off_y) % 4 * 4 + (chip_x + off_x) % 4

    peers = []
    same_core = []
    unheard = []
    for off_x, off_y in OFFSETS:
        chip = chip_of(off_x, off_y)
        both = [chip * 2 + core, chip * 2 + 1 - core]
        peers += both
        same_core += both[:1]
        if off_y != 0:
            unheard += both if off_x != 0 else both[1:]
    peers.append(sibling)

    def send_blocks(targets, stage, recv, send_sem, recv_sem):
        for target in targets:
            pltpu.make_async_remote_copy(
                src_ref=stage.at[target],
                dst_ref=recv.at[me],
                send_sem=send_sem,
                recv_sem=recv_sem,
                device_id={"dap": target},
                device_id_type=MESH,
            ).start()

    pending = []

    def exchange(stage, recv, send_sem, recv_sem):
        send_blocks(peers, stage, recv, send_sem, recv_sem)
        pltpu.make_async_copy(stage.at[me], recv.at[me], recv_sem).start()
        pending.append((stage.at[pl.ds(0, DAP - 1)], send_sem))

    def weight_sends(source, dest, index):
        def send(step, carry):
            target = (my_dp + step) % dp_count
            pltpu.make_async_remote_copy(
                src_ref=source,
                dst_ref=dest.at[my_dp],
                send_sem=w_send.at[index],
                recv_sem=w_recv.at[index],
                device_id={"dp": target},
                device_id_type=MESH,
            ).start()
            return carry

        lax.fori_loop(1, dp_count, send, 0)
        pltpu.make_async_copy(source, dest.at[my_dp], w_recv.at[index]).start()
        pending.append((dest.at[pl.ds(0, dp_count - 1)], w_send.at[index]))

    load_x = pltpu.make_async_copy(x_hbm, x_ref, load_sems.at[0])
    load_x.start()
    load_tri = pltpu.make_async_copy(tri_project_ref, tri_in, load_sems.at[7])
    load_tri.start()
    loads = [
        pltpu.make_async_copy(tri_gate_ref, mix_stage.at[0, :, 0:128], load_sems.at[1]),
        pltpu.make_async_copy(tri_output_ref, mix_stage.at[0, :, 128:256], load_sems.at[2]),
        pltpu.make_async_copy(
            attn_project_ref.at[:, 0:256], mix_stage.at[0, :, 256:512], load_sems.at[3]
        ),
        pltpu.make_async_copy(
            attn_project_ref.at[:, 256:512], mix_stage.at[1, :, 0:256], load_sems.at[6]
        ),
        pltpu.make_async_copy(attn_output_ref, mix_stage.at[1, :, 256:384], load_sems.at[4]),
        pltpu.make_async_copy(attn_bias_ref, bias_in, load_sems.at[5]),
    ]
    for load in loads:
        load.start()

    def relay(weights, index):
        wait_bytes(weights.at[0], w_recv.at[index])
        pltpu.make_async_remote_copy(
            src_ref=weights.at[core],
            dst_ref=weights.at[core],
            send_sem=relay_send.at[index],
            recv_sem=relay_recv.at[index],
            device_id={"dap": sibling},
            device_id_type=MESH,
        ).start()
        pending.append((weights.at[0], relay_send.at[index]))

    barrier = pltpu.get_barrier_semaphore()

    for step in range(1, dp_count):
        pl.semaphore_signal(
            barrier,
            inc=1,
            device_id={"dp": (my_dp + step) % dp_count},
            device_id_type=MESH,
        )
    column_chips = [chip_of(0, off) * 2 + core for off in (2, 1, 3)]
    row_group = []
    for off in (2, 1, 3):
        row_group += [chip_of(off, 0) * 2 + core, chip_of(off, 0) * 2 + 1 - core]
    for target in column_chips + row_group + [sibling]:
        pl.semaphore_signal(barrier, inc=1, device_id={"dap": target}, device_id_type=MESH)

    load_tri.wait()
    tri_whole = tri_in[...].astype(F32)
    for quarter in range(PARTS):
        tri_stage[quarter] = jnp.concatenate(
            [
                tri_whole[:, part * C + quarter * PART : part * C + (quarter + 1) * PART]
                for part in range(4)
            ],
            axis=1,
        ).astype(BF16)

    load_x.wait()

    def cut_pair(two, carry):
        start = pl.multiple_of(two * 16, 16)
        both = x_ref[0, :, pl.ds(start, 16), :].astype(F32)
        pair_stage[two * 2] = both[:, :8].reshape(64, C).astype(BF16)
        pair_stage[two * 2 + 1] = both[:, 8:].reshape(64, C).astype(BF16)
        return carry

    lax.fori_loop(0, DAP // 2, cut_pair, 0, unroll=2)

    def norm_row(row, carry):
        normed_rows[row] = norm_over(x_ref[0, row].astype(F32), 1).astype(BF16)
        return carry

    lax.fori_loop(0, ROWS, norm_row, 0, unroll=2)
    pl.semaphore_wait(barrier, dp_count - 1 + 10)

    for target in column_chips:
        pl.semaphore_signal(ready_sem, inc=1, device_id={"dap": target}, device_id_type=MESH)
    weight_sends(tri_stage.at[0], w_tri.at[0], 4)
    heard = row_group + column_chips + [sibling]
    send_blocks(heard, pair_stage, pair_recv, pair_sems.at[0], pair_sems.at[1])

    for quarter in range(1, PARTS):
        weight_sends(tri_stage.at[quarter], w_tri.at[quarter], 4 + quarter)
    pl.semaphore_wait(ready_sem, 3)
    send_blocks(unheard, pair_stage, pair_recv, pair_sems.at[0], pair_sems.at[1])
    pltpu.make_async_copy(pair_stage.at[me], pair_recv.at[me], pair_sems.at[1]).start()
    pending.append((pair_stage.at[pl.ds(0, DAP - 1)], pair_sems.at[0]))

    length = length_ref[0]
    valid_cols = (lax.broadcasted_iota(jnp.int32, (1, TOKENS), 1) < length).astype(F32)

    for quarter in range(PARTS):
        wait_bytes(w_tri.at[quarter], w_recv.at[4 + quarter])
        wt_tri[quarter] = transposed(w_tri[quarter].reshape(C, C))

        def project_row(row, carry):
            valid_row = (me * ROWS + row < length).astype(F32)
            mask = valid_cols * valid_row
            projected = dot(wt_tri[quarter], normed_rows[row], NT)
            for side in range(2):
                gate = projected[2 * side * PART : (2 * side + 1) * PART]
                value = projected[(2 * side + 1) * PART : (2 * side + 2) * PART]
                kept = sigmoid(gate) * value * mask
                lr_rows[side, 0, pl.ds(row, PART, stride=ROWS), :] = kept[:, :128]
                lr_rows[side, 1, pl.ds(row, PART, stride=ROWS), :] = kept[:, 128:]
            return carry

        lax.fori_loop(0, ROWS, project_row, 0, unroll=4)
        for lanes in range(2):
            lr_stage[quarter, :, :, lanes * 128 : (lanes + 1) * 128] = jnp.concatenate(
                [lr_rows[side, lanes].reshape(DAP, ROWS, 128) for side in range(2)], axis=1
            ).astype(BF16)
        exchange(
            lr_stage.at[quarter],
            lr_recv.at[quarter],
            lr_send.at[quarter],
            lr_recv_sem.at[quarter],
        )
        if quarter > 0:
            continue

        for load in loads:
            load.wait()
        slice_rows = mix_stage.shape[1]
        bias_square[...] = jnp.zeros((C, C), F32)
        bias_square[0:HEADS, 0:slice_rows] = bias_in[...].astype(F32)
        mix_stage[1, :, 384:512] = jnp.transpose(bias_square[...])[0:slice_rows].astype(BF16)
        lanes = pl.ds(pl.multiple_of(core * FF, FF), FF)
        rows_sent = reduce_ref.shape[0] // 2
        rows = pl.ds(pl.multiple_of(core * rows_sent, rows_sent), rows_sent)
        weight_sends(mix_stage.at[core], w_mix.at[core], 1)
        weight_sends(expand_ref.at[:, lanes], w_expand.at[core], 2)
        weight_sends(reduce_ref.at[rows, :], w_reduce.at[core], 3)

    relay(w_mix, 1)
    wait_bytes(pair_recv, pair_sems.at[1])
    x_cols[...] = pair_recv[...].astype(F32).reshape(TOKENS * ROWS, C)

    wait_bytes(w_mix.at[0], relay_recv.at[1])
    for part in range(8):
        wt_mix[part] = transposed(
            w_mix[part // 4, :, :, (part % 4) * C : (part % 4 + 1) * C].reshape(C, C)
        )

    def column_gate(col, carry):
        column = jnp.transpose(x_cols[pl.ds(col, TOKENS, stride=ROWS), :])
        xt[col] = column
        normed = norm_over(column, 0).astype(BF16)
        gate_t[col] = sigmoid(dot(wt_mix[0], normed, NN))
        return carry

    lax.fori_loop(0, ROWS, column_gate, 0, unroll=2)
    v_aug[...] = jnp.ones(v_aug.shape, BF16)
    q_diag[...] = jnp.zeros(q_diag.shape, BF16)

    for quarter in range(PARTS):
        wait_bytes(lr_recv.at[quarter], lr_recv_sem.at[quarter])
        both = lr_recv[quarter].astype(F32)
        left = both[:, :ROWS].reshape(TOKENS, TOKENS).astype(BF16)
        right = both[:, ROWS:].reshape(TOKENS, TOKENS).astype(BF16)
        total = dot(right, left, NT)
        c_stage[quarter] = jnp.concatenate(
            [
                total[:, :128].reshape(DAP, ROWS, 128),
                total[:, 128:].reshape(DAP, ROWS, 128),
            ],
            axis=1,
        ).astype(BF16)
        exchange(
            c_stage.at[quarter],
            c_recv.at[quarter],
            c_send.at[quarter],
            c_recv_sem.at[quarter],
        )
        if quarter == 1:
            relay(w_expand, 2)
        if quarter == 2:
            relay(w_reduce, 3)

    wait_bytes(w_expand.at[0], relay_recv.at[2])
    for part in range(8):
        wt_expand[part * C : (part + 1) * C] = transposed(
            w_expand[part // 4, :, :, (part % 4) * C : (part % 4 + 1) * C].reshape(C, C)
        )
    wait_bytes(w_reduce.at[0], relay_recv.at[3])
    blocks = [(half, index) for index in range(dp_count) for half in range(2)]
    for part in range(FF // C):
        own = blocks[part * len(blocks) * C // FF : (part + 1) * len(blocks) * C // FF]
        wt_reduce[:, part * C : (part + 1) * C] = transposed(
            jnp.concatenate([w_reduce[half, index] for half, index in own], axis=0)
        )

    means = []
    squares = []
    zero = jnp.zeros((16, 128), F32)
    for quarter in range(PARTS):
        wait_bytes(c_recv.at[quarter], c_recv_sem.at[quarter])

        def c_sum(step, total):
            for inner in range(4):
                block = step * 4 + inner
                value = c_recv[quarter, block].astype(F32)
                start = pl.multiple_of((quarter * PART + block) * ROWS, ROWS)
                c_values[0, pl.ds(start, ROWS), :] = value[:ROWS]
                c_values[1, pl.ds(start, ROWS), :] = value[ROWS:]
                total = total + value
            return total

        mean = lax.fori_loop(0, PART // 4, c_sum, zero) * (1.0 / PART)

        def c_square(step, total):
            for inner in range(4):
                apart = c_recv[quarter, step * 4 + inner].astype(F32) - mean
                total = total + apart * apart
            return total

        means.append(mean)
        squares.append(lax.fori_loop(0, PART // 4, c_square, zero))
    mean = sum(means) * (1.0 / PARTS)
    variance = sum(
        square + (own - mean) * (own - mean) * PART for square, own in zip(squares, means)
    ) * (1.0 / C)
    scale = lax.rsqrt(variance + EPS)
    c_mean[...] = jnp.concatenate([mean[:ROWS], mean[ROWS:]], axis=1)
    c_scale[...] = jnp.concatenate([scale[:ROWS], scale[ROWS:]], axis=1)

    def column_first(col, carry):
        values = jnp.concatenate(
            [
                c_values[0, pl.ds(col, C, stride=ROWS), :],
                c_values[1, pl.ds(col, C, stride=ROWS), :],
            ],
            axis=1,
        )
        normed = ((values - c_mean[pl.ds(col, 1), :]) * c_scale[pl.ds(col, 1), :]).astype(BF16)
        first = xt[col] + gate_t[col] * dot(wt_mix[1], normed, NN)
        first_t[col] = first
        first_norm = norm_over(first, 0).astype(BF16)
        first_norm_t[col] = first_norm
        bias = dot(wt_mix[7, 0:16], first_norm, NN)[:8]
        slot = col // GROUP
        inner = col - slot * GROUP
        bias_rows[slot, 0, pl.ds(inner, 8, stride=GROUP), :] = bias[:, :128]
        bias_rows[slot, 1, pl.ds(inner, 8, stride=GROUP), :] = bias[:, 128:]
        return carry

    for half in range(2):
        lax.fori_loop(half * GROUP, (half + 1) * GROUP, column_first, 0, unroll=4)
        for lanes in range(2):
            bias_stage[half, :, lanes * 128 : (lanes + 1) * 128] = bias_rows[
                half, lanes, 0 : HEADS * GROUP
            ].astype(BF16)
        for target in same_core:
            pltpu.make_async_remote_copy(
                src_ref=bias_stage.at[half],
                dst_ref=bias_recv.at[half, core, my_chip],
                send_sem=bias_send.at[half],
                recv_sem=bias_recv_sem.at[half],
                device_id={"dap": target},
                device_id_type=MESH,
            ).start()
        pltpu.make_async_copy(
            bias_stage.at[half], bias_recv.at[half, core, my_chip], bias_recv_sem.at[half]
        ).start()
        pending.append((bias_recv.at[half, 0, pl.ds(0, DAP // 2 - 1)], bias_send.at[half]))

    def relay_bias(half):
        wait_bytes(bias_recv.at[half, 0], bias_recv_sem.at[half])
        pltpu.make_async_remote_copy(
            src_ref=bias_recv.at[half, core],
            dst_ref=bias_recv.at[half, core],
            send_sem=bias_relay_send.at[half],
            recv_sem=bias_relay_recv.at[half],
            device_id={"dap": sibling},
            device_id_type=MESH,
        ).start()
        pending.append((bias_recv.at[half, 0], bias_relay_send.at[half]))

    q_scale = LOG2E / HEAD**0.5

    def column_project(col, carry):
        first_norm = first_norm_t[col]
        query = (dot(wt_mix[2], first_norm, NN) * q_scale).astype(BF16)
        value = dot(wt_mix[4], first_norm, NN).astype(BF16)
        og_t[col] = sigmoid(dot(wt_mix[5], first_norm, NN))
        k_cols[col] = transposed(dot(wt_mix[3], first_norm, NN))
        for head in range(HEADS):
            rows = slice(head * HEAD, (head + 1) * HEAD)
            q_diag[col, rows, head * TOKENS : (head + 1) * TOKENS] = query[rows]
            v_aug[col, head, 0:HEAD, :] = value[rows]
        return carry

    lax.fori_loop(0, ROWS, column_project, 0, unroll=2)

    relay_bias(0)
    def column_scores(col, carry):
        for head in range(HEADS):
            lanes = slice(head * TOKENS, (head + 1) * TOKENS)
            scores_ref[col, :, lanes] = dot(k_cols[col], q_diag[col, :, lanes], NN)
        return carry

    lax.fori_loop(0, ROWS, column_scores, 0)
    relay_bias(1)
    for half in range(2):
        wait_bytes(bias_recv.at[half, 0], bias_relay_recv.at[half])
    masked = jnp.where(
        lax.broadcasted_iota(jnp.int32, (TOKENS, TOKENS), 0) < length, 0.0, -1e9
    )
    for pair in range(HEADS // 2):
        tiles = []
        for half in range(2):
            by_core = bias_recv[half].astype(F32)[:, :, pair * 8 : pair * 8 + 8]
            by_chip = [by_core[own, chip] for chip in range(DAP // 2) for own in range(2)]
            tiles.append(jnp.stack(by_chip, axis=0))
        low = lax.broadcasted_iota(jnp.int32, (DAP, 8, TOKENS), 1) < GROUP
        swapped = [pltpu.roll(tile, GROUP, 1) for tile in tiles]
        heads = (
            jnp.where(low, tiles[0], swapped[1]),
            jnp.where(low, swapped[0], tiles[1]),
        )
        for inner in range(2):
            turned = jnp.transpose(heads[inner].reshape(TOKENS, TOKENS))
            head = pair * 2 + inner
            bias_t[:, head * TOKENS : (head + 1) * TOKENS] = turned * LOG2E + masked

    def attend(two):
        seconds = []
        for col in (two * 2, two * 2 + 1):
            scores = [
                scores_ref[col, :, head * TOKENS : (head + 1) * TOKENS]
                + bias_t[:, head * TOKENS : (head + 1) * TOKENS]
                for head in range(HEADS)
            ]
            softs = [
                jnp.exp2(score - jnp.max(score, axis=0, keepdims=True)).astype(BF16)
                for score in scores
            ]
            sums = [dot(v_aug[col, head], softs[head], NN) for head in range(HEADS)]
            attended = jnp.concatenate(
                [total[0:HEAD] * (1.0 / total[HEAD : HEAD + 1]) for total in sums], axis=0
            )
            gated = (attended * og_t[col]).astype(BF16)
            seconds.append(first_t[col] + dot(wt_mix[6], gated, NN))
        return seconds

    def transition(two, seconds):
        norms = [norm_over(second, 0).astype(BF16) for second in seconds]
        hiddens = [dot(wt_expand[0:FF], norm, NN) for norm in norms]
        ups = [dot(wt_expand[FF : 2 * FF], norm, NN) for norm in norms]
        activated = [
            (hidden * sigmoid(hidden) * up).astype(BF16) for hidden, up in zip(hiddens, ups)
        ]
        results = [
            jnp.transpose(second + dot(wt_reduce[...], act, NN)).reshape(DAP, ROWS, C)
            for second, act in zip(seconds, activated)
        ]
        out_stage[two] = jnp.concatenate(results, axis=1).astype(BF16)

    def send_out(two):
        exchange(out_stage.at[two], out_recv.at[two], out_send.at[two], out_recv_sem.at[two])
        pending.pop()

    second_t[0], second_t[1] = attend(0)

    def column_attend(two, carry):
        before = [second_t[0], second_t[1]]
        transition(two - 1, before)
        after = attend(two)
        send_out(two - 1)
        second_t[0], second_t[1] = after
        return carry

    lax.fori_loop(1, ROWS // 2, column_attend, 0)
    transition(ROWS // 2 - 1, [second_t[0], second_t[1]])
    send_out(ROWS // 2 - 1)

    for two in range(ROWS // 2):
        wait_bytes(out_recv.at[two], out_recv_sem.at[two])

    for two in range(ROWS // 2):
        wait_bytes(out_stage.at[two, pl.ds(0, DAP - 1)], out_send.at[two])
    for ref, sem in pending:
        wait_bytes(ref, sem)


def to_rows(blocks_ref, out_ref, blocks, wide, rows, load_sems, store_sems):
    loads = [
        pltpu.make_async_copy(blocks_ref.at[two], blocks.at[two], load_sems.at[two])
        for two in range(ROWS // 2)
    ]
    for load in loads:
        load.start()
    for two, load in enumerate(loads):
        load.wait()
        wide[:, two * 16 : (two + 1) * 16] = blocks[two].astype(F32)
    flat = wide.reshape(TOKENS * ROWS, C)
    stores = []
    for row in range(ROWS):
        rows[row] = flat[pl.ds(row, TOKENS, stride=ROWS), :].astype(BF16)
        stores.append(pltpu.make_async_copy(rows.at[row], out_ref.at[0, row], store_sems.at[row]))
        stores[-1].start()
    for store in stores:
        store.wait()


def fused(dp_count, pair_repr, lengths, *weights):
    slice_rows = C // dp_count
    anywhere = pl.BlockSpec(memory_space=pltpu.HBM)
    scratch = [
        pltpu.VMEM((1, ROWS, TOKENS, C), BF16),
        pltpu.VMEM((HEADS, slice_rows), BF16),
        pltpu.VMEM((C, C), F32),
        pltpu.VMEM((slice_rows, 4 * C), BF16),
        pltpu.VMEM((PARTS, slice_rows, C), BF16),
        pltpu.VMEM((2, slice_rows, FF), BF16),
        pltpu.VMEM((PARTS, dp_count, slice_rows, C), BF16),
        pltpu.VMEM((2, dp_count, slice_rows, FF), BF16),
        pltpu.VMEM((2, dp_count, slice_rows, FF), BF16),
        pltpu.VMEM((2, dp_count, FF // dp_count // 2, C), BF16),
        pltpu.VMEM((PARTS, C, C), BF16),
        pltpu.VMEM((8, C, C), BF16),
        pltpu.VMEM((2 * FF, C), BF16),
        pltpu.VMEM((C, FF), BF16),
        pltpu.VMEM((DAP, 64, C), BF16),
        pltpu.VMEM((DAP, 64, C), BF16),
        pltpu.VMEM((ROWS, TOKENS, C), BF16),
        pltpu.VMEM((2, 2, PART * ROWS, 128), F32),
        pltpu.VMEM((PARTS, DAP, 16, TOKENS), BF16),
        pltpu.VMEM((PARTS, DAP, 16, TOKENS), BF16),
        pltpu.VMEM((PARTS, DAP, 16, 128), BF16),
        pltpu.VMEM((PARTS, DAP, 16, 128), BF16),
        pltpu.VMEM((2, C * ROWS, 128), F32),
        pltpu.VMEM((ROWS, TOKENS), F32),
        pltpu.VMEM((ROWS, TOKENS), F32),
        pltpu.VMEM((TOKENS * ROWS, C), F32),
        pltpu.VMEM((ROWS, C, TOKENS), F32),
        pltpu.VMEM((ROWS, C, TOKENS), F32),
        pltpu.VMEM((ROWS, C, TOKENS), F32),
        pltpu.VMEM((ROWS, C, TOKENS), BF16),
        pltpu.VMEM((2, 2, 8 * GROUP, 128), F32),
        pltpu.VMEM((2, HEADS * GROUP, TOKENS), BF16),
        pltpu.VMEM((2, 2, DAP // 2, HEADS * GROUP, TOKENS), BF16),
        pltpu.VMEM((TOKENS, HEADS * TOKENS), F32),
        pltpu.VMEM((ROWS, C, HEADS * TOKENS), BF16),
        pltpu.VMEM((ROWS, TOKENS, C), BF16),
        pltpu.VMEM((ROWS, HEADS, 48, TOKENS), BF16),
        pltpu.VMEM((ROWS, C, TOKENS), F32),
        pltpu.VMEM((ROWS, TOKENS, HEADS * TOKENS), F32),
        pltpu.VMEM((2, C, TOKENS), F32),
        pltpu.VMEM((ROWS // 2, DAP, 16, C), BF16),
        pltpu.SemaphoreType.DMA((4 + PARTS,)),
        pltpu.SemaphoreType.DMA((4 + PARTS,)),
        pltpu.SemaphoreType.DMA((4,)),
        pltpu.SemaphoreType.DMA((4,)),
        pltpu.SemaphoreType.DMA((2,)),
        pltpu.SemaphoreType.DMA((PARTS,)),
        pltpu.SemaphoreType.DMA((PARTS,)),
        pltpu.SemaphoreType.DMA((PARTS,)),
        pltpu.SemaphoreType.DMA((PARTS,)),
        pltpu.SemaphoreType.DMA((2,)),
        pltpu.SemaphoreType.DMA((2,)),
        pltpu.SemaphoreType.DMA((2,)),
        pltpu.SemaphoreType.DMA((2,)),
        pltpu.SemaphoreType.DMA((ROWS // 2,)),
        pltpu.SemaphoreType.DMA((ROWS // 2,)),
        pltpu.SemaphoreType.DMA((8,)),
        pltpu.SemaphoreType.REGULAR,
    ]
    blocks = pl.pallas_call(
        functools.partial(body, dp_count),
        out_shape=jax.ShapeDtypeStruct((ROWS // 2, DAP, 16, C), BF16),
        in_specs=[pl.BlockSpec(memory_space=pltpu.SMEM)] + [anywhere] * 9,
        out_specs=anywhere,
        scratch_shapes=scratch,
        compiler_params=pltpu.CompilerParams(
            collective_id=0, has_side_effects=True, vmem_limit_bytes=VMEM_LIMIT
        ),
    )(lengths, pair_repr, *weights[:4], jnp.transpose(weights[4]), *weights[5:])
    return pl.pallas_call(
        to_rows,
        out_shape=jax.ShapeDtypeStruct((1, ROWS, TOKENS, C), BF16),
        in_specs=[anywhere],
        out_specs=anywhere,
        scratch_shapes=[
            pltpu.VMEM((ROWS // 2, DAP, 16, C), BF16),
            pltpu.VMEM((DAP, 64, C), F32),
            pltpu.VMEM((ROWS, TOKENS, C), BF16),
            pltpu.SemaphoreType.DMA((ROWS // 2,)),
            pltpu.SemaphoreType.DMA((ROWS,)),
        ],
        compiler_params=pltpu.CompilerParams(vmem_limit_bytes=VMEM_LIMIT),
    )(blocks)


def solution(mesh):
    dp_count = mesh.shape["dp"]
    placed = (P("dp", "dap", None, None), P("dp")) + (P("dp", None),) * 8
    return jax.shard_map(
        functools.partial(fused, dp_count),
        mesh=mesh,
        in_specs=placed,
        out_specs=P("dp", "dap", None, None),
        check_vma=False,
    )
```

```python
import functools

import jax
import jax.numpy as jnp
from jax import lax
from jax.experimental import pallas as pl
from jax.experimental.pallas import tpu as pltpu
from jax.sharding import PartitionSpec as P

F32 = jnp.float32
BF16 = jnp.bfloat16
NN = (((1,), (0,)), ((), ()))
NT = (((1,), (1,)), ((), ()))
TN = (((0,), (0,)), ((), ()))
LOG2E = 1.4426950408889634
EPS = 1e-05

ROWS = 8
TOKENS = 256
C = 128
HEADS = 4
HEAD = 32
FF = 512
VMEM_LIMIT = 64 * 1024 * 1024 - 65536
DAP = TOKENS // ROWS
PARTS = 4
PART = C // PARTS
GROUP = ROWS // 2


OFFSETS = (
    (2, 2), (2, 3), (3, 2), (2, 1), (1, 2), (0, 2), (2, 0), (3, 1),
    (1, 3), (3, 3), (1, 1), (0, 3), (3, 0), (0, 1), (1, 0),
)
MESH = pl.DeviceIdType.MESH


def dot(left, right, dims):
    return lax.dot_general(left, right, dims, preferred_element_type=F32)


def sigmoid(v):
    return 0.5 + 0.5 * jnp.tanh(0.5 * v)


def norm_over(values, axis):
    mean = jnp.mean(values, axis=axis, keepdims=True)
    centred = values - mean
    variance = jnp.mean(centred * centred, axis=axis, keepdims=True)
    return centred * lax.rsqrt(variance + EPS)


def transposed(value):
    return jnp.transpose(value.astype(F32)).astype(BF16)


def wait_bytes(ref, sem):
    pltpu.make_async_copy(ref, ref, sem).wait()


def body(
    dp_count,
    length_ref,
    x_hbm,
    tri_project_ref,
    tri_gate_ref,
    tri_output_ref,
    attn_project_ref,
    attn_bias_ref,
    attn_output_ref,
    expand_ref,
    reduce_ref,
    out_recv,
    x_ref,
    bias_in,
    bias_square,
    tri_in,
    tri_stage,
    mix_stage,
    w_tri,
    w_mix,
    w_expand,
    w_reduce,
    wt_tri,
    wt_mix,
    wt_expand,
    wt_reduce,
    pair_stage,
    pair_recv,
    normed_rows,
    lr_rows,
    lr_stage,
    lr_recv,
    c_stage,
    c_recv,
    c_values,
    c_mean,
    c_scale,
    x_cols,
    xt,
    gate_t,
    first_t,
    first_norm_t,
    bias_rows,
    bias_stage,
    bias_recv,
    bias_t,
    q_diag,
    k_cols,
    v_aug,
    og_t,
    scores_ref,
    second_t,
    out_stage,
    w_send,
    w_recv,
    relay_send,
    relay_recv,
    pair_sems,
    lr_send,
    lr_recv_sem,
    c_send,
    c_recv_sem,
    bias_send,
    bias_recv_sem,
    bias_relay_send,
    bias_relay_recv,
    out_send,
    out_recv_sem,
    load_sems,
    ready_sem,
):
    me = lax.axis_index("dap")
    my_dp = lax.axis_index("dp")
    core = me % 2
    my_chip = me // 2
    chip_x = (me // 2) % 4
    chip_y = me // 8

    sibling = me + 1 - 2 * core

    def chip_of(off_x, off_y):
        return (chip_y + off_y) % 4 * 4 + (chip_x + off_x) % 4

    peers = []
    same_core = []
    unheard = []
    for off_x, off_y in OFFSETS:
        chip = chip_of(off_x, off_y)
        both = [chip * 2 + core, chip * 2 + 1 - core]
        peers += both
        same_core += both[:1]
        if off_y != 0:
            unheard += both if off_x != 0 else both[1:]
    peers.append(sibling)

    def send_blocks(targets, stage, recv, send_sem, recv_sem):
        for target in targets:
            pltpu.make_async_remote_copy(
                src_ref=stage.at[target],
                dst_ref=recv.at[me],
                send_sem=send_sem,
                recv_sem=recv_sem,
                device_id={"dap": target},
                device_id_type=MESH,
            ).start()

    pending = []

    def exchange(stage, recv, send_sem, recv_sem):
        send_blocks(peers, stage, recv, send_sem, recv_sem)
        pltpu.make_async_copy(stage.at[me], recv.at[me], recv_sem).start()
        pending.append((stage.at[pl.ds(0, DAP - 1)], send_sem))

    def weight_sends(source, dest, index):
        def send(step, carry):
            target = (my_dp + step) % dp_count
            pltpu.make_async_remote_copy(
                src_ref=source,
                dst_ref=dest.at[my_dp],
                send_sem=w_send.at[index],
                recv_sem=w_recv.at[index],
                device_id={"dp": target},
                device_id_type=MESH,
            ).start()
            return carry

        lax.fori_loop(1, dp_count, send, 0)
        pltpu.make_async_copy(source, dest.at[my_dp], w_recv.at[index]).start()
        pending.append((dest.at[pl.ds(0, dp_count - 1)], w_send.at[index]))

    load_x = pltpu.make_async_copy(x_hbm, x_ref, load_sems.at[0])
    load_x.start()
    load_tri = pltpu.make_async_copy(tri_project_ref, tri_in, load_sems.at[7])
    load_tri.start()
    loads = [
        pltpu.make_async_copy(tri_gate_ref, mix_stage.at[0, :, 0:128], load_sems.at[1]),
        pltpu.make_async_copy(tri_output_ref, mix_stage.at[0, :, 128:256], load_sems.at[2]),
        pltpu.make_async_copy(
            attn_project_ref.at[:, 0:256], mix_stage.at[0, :, 256:512], load_sems.at[3]
        ),
        pltpu.make_async_copy(
            attn_project_ref.at[:, 256:512], mix_stage.at[1, :, 0:256], load_sems.at[6]
        ),
        pltpu.make_async_copy(attn_output_ref, mix_stage.at[1, :, 256:384], load_sems.at[4]),
        pltpu.make_async_copy(attn_bias_ref, bias_in, load_sems.at[5]),
    ]
    for load in loads:
        load.start()

    def relay(weights, index):
        wait_bytes(weights.at[0], w_recv.at[index])
        pltpu.make_async_remote_copy(
            src_ref=weights.at[core],
            dst_ref=weights.at[core],
            send_sem=relay_send.at[index],
            recv_sem=relay_recv.at[index],
            device_id={"dap": sibling},
            device_id_type=MESH,
        ).start()
        pending.append((weights.at[0], relay_send.at[index]))

    barrier = pltpu.get_barrier_semaphore()

    for step in range(1, dp_count):
        pl.semaphore_signal(
            barrier,
            inc=1,
            device_id={"dp": (my_dp + step) % dp_count},
            device_id_type=MESH,
        )
    column_chips = [chip_of(0, off) * 2 + core for off in (2, 1, 3)]
    row_group = []
    for off in (2, 1, 3):
        row_group += [chip_of(off, 0) * 2 + core, chip_of(off, 0) * 2 + 1 - core]
    for target in column_chips + row_group + [sibling]:
        pl.semaphore_signal(barrier, inc=1, device_id={"dap": target}, device_id_type=MESH)

    load_tri.wait()
    tri_whole = tri_in[...].astype(F32)
    for quarter in range(PARTS):
        tri_stage[quarter] = jnp.concatenate(
            [
                tri_whole[:, part * C + quarter * PART : part * C + (quarter + 1) * PART]
                for part in range(4)
            ],
            axis=1,
        ).astype(BF16)

    load_x.wait()

    def cut_pair(two, carry):
        start = pl.multiple_of(two * 16, 16)
        both = x_ref[0, :, pl.ds(start, 16), :].astype(F32)
        pair_stage[two * 2] = both[:, :8].reshape(64, C).astype(BF16)
        pair_stage[two * 2 + 1] = both[:, 8:].reshape(64, C).astype(BF16)
        return carry

    lax.fori_loop(0, DAP // 2, cut_pair, 0, unroll=2)

    def norm_row(row, carry):
        normed_rows[row] = norm_over(x_ref[0, row].astype(F32), 1).astype(BF16)
        return carry

    lax.fori_loop(0, ROWS, norm_row, 0, unroll=2)
    pl.semaphore_wait(barrier, dp_count - 1 + 10)

    for target in column_chips:
        pl.semaphore_signal(ready_sem, inc=1, device_id={"dap": target}, device_id_type=MESH)
    weight_sends(tri_stage.at[0], w_tri.at[0], 4)
    heard = row_group + column_chips + [sibling]
    send_blocks(heard, pair_stage, pair_recv, pair_sems.at[0], pair_sems.at[1])

    for quarter in range(1, PARTS):
        weight_sends(tri_stage.at[quarter], w_tri.at[quarter], 4 + quarter)
    pl.semaphore_wait(ready_sem, 3)
    send_blocks(unheard, pair_stage, pair_recv, pair_sems.at[0], pair_sems.at[1])
    pltpu.make_async_copy(pair_stage.at[me], pair_recv.at[me], pair_sems.at[1]).start()
    pending.append((pair_stage.at[pl.ds(0, DAP - 1)], pair_sems.at[0]))

    length = length_ref[0]
    valid_cols = (lax.broadcasted_iota(jnp.int32, (1, TOKENS), 1) < length).astype(F32)

    for quarter in range(PARTS):
        wait_bytes(w_tri.at[quarter], w_recv.at[4 + quarter])
        wt_tri[quarter] = transposed(w_tri[quarter].reshape(C, C))

        def project_row(row, carry):
            valid_row = (me * ROWS + row < length).astype(F32)
            mask = valid_cols * valid_row
            projected = dot(wt_tri[quarter], normed_rows[row], NT)
            for side in range(2):
                gate = projected[2 * side * PART : (2 * side + 1) * PART]
                value = projected[(2 * side + 1) * PART : (2 * side + 2) * PART]
                kept = sigmoid(gate) * value * mask
                lr_rows[side, 0, pl.ds(row, PART, stride=ROWS), :] = kept[:, :128]
                lr_rows[side, 1, pl.ds(row, PART, stride=ROWS), :] = kept[:, 128:]
            return carry

        lax.fori_loop(0, ROWS, project_row, 0, unroll=8)
        for lanes in range(2):
            lr_stage[quarter, :, :, lanes * 128 : (lanes + 1) * 128] = jnp.concatenate(
                [lr_rows[side, lanes].reshape(DAP, ROWS, 128) for side in range(2)], axis=1
            ).astype(BF16)
        exchange(
            lr_stage.at[quarter],
            lr_recv.at[quarter],
            lr_send.at[quarter],
            lr_recv_sem.at[quarter],
        )
        if quarter > 0:
            continue

        for load in loads:
            load.wait()
        slice_rows = mix_stage.shape[1]
        bias_square[...] = jnp.zeros((C, C), F32)
        bias_square[0:HEADS, 0:slice_rows] = bias_in[...].astype(F32)
        mix_stage[1, :, 384:512] = jnp.transpose(bias_square[...])[0:slice_rows].astype(BF16)
        lanes = pl.ds(pl.multiple_of(core * FF, FF), FF)
        rows_sent = reduce_ref.shape[0] // 2
        rows = pl.ds(pl.multiple_of(core * rows_sent, rows_sent), rows_sent)
        weight_sends(mix_stage.at[core], w_mix.at[core], 1)
        weight_sends(expand_ref.at[:, lanes], w_expand.at[core], 2)
        weight_sends(reduce_ref.at[rows, :], w_reduce.at[core], 3)

    relay(w_mix, 1)
    wait_bytes(pair_recv, pair_sems.at[1])
    x_cols[...] = pair_recv[...].astype(F32).reshape(TOKENS * ROWS, C)

    wait_bytes(w_mix.at[0], relay_recv.at[1])
    for part in range(8):
        wt_mix[part] = transposed(
            w_mix[part // 4, :, :, (part % 4) * C : (part % 4 + 1) * C].reshape(C, C)
        )

    def column_gate(col, carry):
        column = jnp.transpose(x_cols[pl.ds(col, TOKENS, stride=ROWS), :])
        xt[col] = column
        normed = norm_over(column, 0).astype(BF16)
        gate_t[col] = sigmoid(dot(wt_mix[0], normed, NN))
        return carry

    lax.fori_loop(0, ROWS, column_gate, 0, unroll=4)
    v_aug[...] = jnp.ones(v_aug.shape, BF16)
    q_diag[...] = jnp.zeros(q_diag.shape, BF16)

    for quarter in range(PARTS):
        wait_bytes(lr_recv.at[quarter], lr_recv_sem.at[quarter])
        both = lr_recv[quarter].astype(F32)
        left = both[:, :ROWS].reshape(TOKENS, TOKENS).astype(BF16)
        right = both[:, ROWS:].reshape(TOKENS, TOKENS).astype(BF16)
        total = dot(right, left, NT)
        c_stage[quarter] = jnp.concatenate(
            [
                total[:, :128].reshape(DAP, ROWS, 128),
                total[:, 128:].reshape(DAP, ROWS, 128),
            ],
            axis=1,
        ).astype(BF16)
        exchange(
            c_stage.at[quarter],
            c_recv.at[quarter],
            c_send.at[quarter],
            c_recv_sem.at[quarter],
        )
        if quarter == 1:
            relay(w_expand, 2)
        if quarter == 2:
            relay(w_reduce, 3)

    wait_bytes(w_expand.at[0], relay_recv.at[2])
    for part in range(8):
        wt_expand[part * C : (part + 1) * C] = transposed(
            w_expand[part // 4, :, :, (part % 4) * C : (part % 4 + 1) * C].reshape(C, C)
        )
    wait_bytes(w_reduce.at[0], relay_recv.at[3])
    blocks = [(half, index) for index in range(dp_count) for half in range(2)]
    for part in range(FF // C):
        own = blocks[part * len(blocks) * C // FF : (part + 1) * len(blocks) * C // FF]
        wt_reduce[:, part * C : (part + 1) * C] = transposed(
            jnp.concatenate([w_reduce[half, index] for half, index in own], axis=0)
        )

    means = []
    squares = []
    zero = jnp.zeros((16, 128), F32)
    for quarter in range(PARTS):
        wait_bytes(c_recv.at[quarter], c_recv_sem.at[quarter])

        def c_sum(step, total):
            for inner in range(4):
                block = step * 4 + inner
                value = c_recv[quarter, block].astype(F32)
                start = pl.multiple_of((quarter * PART + block) * ROWS, ROWS)
                c_values[0, pl.ds(start, ROWS), :] = value[:ROWS]
                c_values[1, pl.ds(start, ROWS), :] = value[ROWS:]
                total = total + value
            return total

        mean = lax.fori_loop(0, PART // 4, c_sum, zero) * (1.0 / PART)

        def c_square(step, total):
            for inner in range(4):
                apart = c_recv[quarter, step * 4 + inner].astype(F32) - mean
                total = total + apart * apart
            return total

        means.append(mean)
        squares.append(lax.fori_loop(0, PART // 4, c_square, zero))
    mean = sum(means) * (1.0 / PARTS)
    variance = sum(
        square + (own - mean) * (own - mean) * PART for square, own in zip(squares, means)
    ) * (1.0 / C)
    scale = lax.rsqrt(variance + EPS)
    c_mean[...] = jnp.concatenate([mean[:ROWS], mean[ROWS:]], axis=1)
    c_scale[...] = jnp.concatenate([scale[:ROWS], scale[ROWS:]], axis=1)

    def column_first(col, carry):
        values = jnp.concatenate(
            [
                c_values[0, pl.ds(col, C, stride=ROWS), :],
                c_values[1, pl.ds(col, C, stride=ROWS), :],
            ],
            axis=1,
        )
        normed = ((values - c_mean[pl.ds(col, 1), :]) * c_scale[pl.ds(col, 1), :]).astype(BF16)
        first = xt[col] + gate_t[col] * dot(wt_mix[1], normed, NN)
        first_t[col] = first
        first_norm = norm_over(first, 0).astype(BF16)
        first_norm_t[col] = first_norm
        bias = dot(wt_mix[7, 0:16], first_norm, NN)[:8]
        slot = col // GROUP
        inner = col - slot * GROUP
        bias_rows[slot, 0, pl.ds(inner, 8, stride=GROUP), :] = bias[:, :128]
        bias_rows[slot, 1, pl.ds(inner, 8, stride=GROUP), :] = bias[:, 128:]
        return carry

    for half in range(2):
        lax.fori_loop(half * GROUP, (half + 1) * GROUP, column_first, 0, unroll=4)
        for lanes in range(2):
            bias_stage[half, :, lanes * 128 : (lanes + 1) * 128] = bias_rows[
                half, lanes, 0 : HEADS * GROUP
            ].astype(BF16)
        for target in same_core:
            pltpu.make_async_remote_copy(
                src_ref=bias_stage.at[half],
                dst_ref=bias_recv.at[half, core, my_chip],
                send_sem=bias_send.at[half],
                recv_sem=bias_recv_sem.at[half],
                device_id={"dap": target},
                device_id_type=MESH,
            ).start()
        pltpu.make_async_copy(
            bias_stage.at[half], bias_recv.at[half, core, my_chip], bias_recv_sem.at[half]
        ).start()
        pending.append((bias_recv.at[half, 0, pl.ds(0, DAP // 2 - 1)], bias_send.at[half]))

    def relay_bias(half):
        wait_bytes(bias_recv.at[half, 0], bias_recv_sem.at[half])
        pltpu.make_async_remote_copy(
            src_ref=bias_recv.at[half, core],
            dst_ref=bias_recv.at[half, core],
            send_sem=bias_relay_send.at[half],
            recv_sem=bias_relay_recv.at[half],
            device_id={"dap": sibling},
            device_id_type=MESH,
        ).start()
        pending.append((bias_recv.at[half, 0], bias_relay_send.at[half]))

    q_scale = LOG2E / HEAD**0.5

    def column_project(col, carry):
        first_norm = first_norm_t[col]
        query = (dot(wt_mix[2], first_norm, NN) * q_scale).astype(BF16)
        value = dot(wt_mix[4], first_norm, NN).astype(BF16)
        og_t[col] = sigmoid(dot(wt_mix[5], first_norm, NN))
        k_cols[col] = transposed(dot(wt_mix[3], first_norm, NN))
        for head in range(HEADS):
            rows = slice(head * HEAD, (head + 1) * HEAD)
            q_diag[col, rows, head * TOKENS : (head + 1) * TOKENS] = query[rows]
            v_aug[col, head, 0:HEAD, :] = value[rows]
        return carry

    lax.fori_loop(0, ROWS, column_project, 0, unroll=4)

    relay_bias(0)
    def column_scores(col, carry):
        for head in range(HEADS):
            lanes = slice(head * TOKENS, (head + 1) * TOKENS)
            scores_ref[col, :, lanes] = dot(k_cols[col], q_diag[col, :, lanes], NN)
        return carry

    lax.fori_loop(0, ROWS, column_scores, 0, unroll=2)
    relay_bias(1)
    for half in range(2):
        wait_bytes(bias_recv.at[half, 0], bias_relay_recv.at[half])
    masked = jnp.where(
        lax.broadcasted_iota(jnp.int32, (TOKENS, TOKENS), 0) < length, 0.0, -1e9
    )
    for pair in range(HEADS // 2):
        tiles = []
        for half in range(2):
            by_core = bias_recv[half].astype(F32)[:, :, pair * 8 : pair * 8 + 8]
            by_chip = [by_core[own, chip] for chip in range(DAP // 2) for own in range(2)]
            tiles.append(jnp.stack(by_chip, axis=0))
        low = lax.broadcasted_iota(jnp.int32, (DAP, 8, TOKENS), 1) < GROUP
        swapped = [pltpu.roll(tile, GROUP, 1) for tile in tiles]
        heads = (
            jnp.where(low, tiles[0], swapped[1]),
            jnp.where(low, swapped[0], tiles[1]),
        )
        for inner in range(2):
            turned = jnp.transpose(heads[inner].reshape(TOKENS, TOKENS))
            head = pair * 2 + inner
            bias_t[:, head * TOKENS : (head + 1) * TOKENS] = turned * LOG2E + masked

    def attend(two):
        seconds = []
        for col in (two * 2, two * 2 + 1):
            scores = [
                scores_ref[col, :, head * TOKENS : (head + 1) * TOKENS]
                + bias_t[:, head * TOKENS : (head + 1) * TOKENS]
                for head in range(HEADS)
            ]
            softs = [
                jnp.exp2(score - jnp.max(score, axis=0, keepdims=True)).astype(BF16)
                for score in scores
            ]
            sums = [dot(v_aug[col, head], softs[head], NN) for head in range(HEADS)]
            attended = jnp.concatenate(
                [total[0:HEAD] * (1.0 / total[HEAD : HEAD + 1]) for total in sums], axis=0
            )
            gated = (attended * og_t[col]).astype(BF16)
            seconds.append(first_t[col] + dot(wt_mix[6], gated, NN))
        return seconds

    def transition(seconds):
        norms = [norm_over(second, 0).astype(BF16) for second in seconds]
        hiddens = [dot(wt_expand[0:FF], norm, NN) for norm in norms]
        ups = [dot(wt_expand[FF : 2 * FF], norm, NN) for norm in norms]
        activated = [
            (hidden * sigmoid(hidden) * up).astype(BF16) for hidden, up in zip(hiddens, ups)
        ]
        results = [
            jnp.transpose(second + dot(wt_reduce[...], act, NN)).reshape(-1, ROWS, C)
            for second, act in zip(seconds, activated)
        ]
        return jnp.concatenate(results, axis=1).astype(BF16)

    def send_out(two):
        exchange(out_stage.at[two], out_recv.at[two], out_send.at[two], out_recv_sem.at[two])
        pending.pop()

    second_t[0], second_t[1] = attend(0)

    def column_attend(two, carry):
        before = [second_t[0], second_t[1]]
        out_stage[two - 1] = transition(before)
        after = attend(two)
        send_out(two - 1)
        second_t[0], second_t[1] = after
        return carry

    lax.fori_loop(1, ROWS // 2, column_attend, 0)
    last = ROWS // 2 - 1
    for half in range(2):
        owners = DAP // 2
        lanes = slice(half * 128, (half + 1) * 128)
        out_stage[last, half * owners : (half + 1) * owners] = transition(
            [second_t[0, :, lanes], second_t[1, :, lanes]]
        )
        targets = [half * owners + (me + step) % owners for step in range(owners)]
        send_blocks(
            targets[1:],
            out_stage.at[last],
            out_recv.at[last],
            out_send.at[last],
            out_recv_sem.at[last],
        )

        @pl.when(me // owners != half)
        def _():
            send_blocks(
                targets[:1],
                out_stage.at[last],
                out_recv.at[last],
                out_send.at[last],
                out_recv_sem.at[last],
            )

    pltpu.make_async_copy(
        out_stage.at[last, me], out_recv.at[last, me], out_recv_sem.at[last]
    ).start()

    for two in range(ROWS // 2):
        wait_bytes(out_recv.at[two], out_recv_sem.at[two])

    for two in range(ROWS // 2):
        wait_bytes(out_stage.at[two, pl.ds(0, DAP - 1)], out_send.at[two])
    for ref, sem in pending:
        wait_bytes(ref, sem)


def to_rows(blocks_ref, out_ref, blocks, wide, rows, load_sems, store_sems):
    loads = [
        pltpu.make_async_copy(blocks_ref.at[two], blocks.at[two], load_sems.at[two])
        for two in range(ROWS // 2)
    ]
    for load in loads:
        load.start()
    for two, load in enumerate(loads):
        load.wait()
        wide[:, two * 16 : (two + 1) * 16] = blocks[two].astype(F32)
    flat = wide.reshape(TOKENS * ROWS, C)
    stores = []
    for row in range(ROWS):
        rows[row] = flat[pl.ds(row, TOKENS, stride=ROWS), :].astype(BF16)
        stores.append(pltpu.make_async_copy(rows.at[row], out_ref.at[0, row], store_sems.at[row]))
        stores[-1].start()
    for store in stores:
        store.wait()


def fused(dp_count, pair_repr, lengths, *weights):
    slice_rows = C // dp_count
    anywhere = pl.BlockSpec(memory_space=pltpu.HBM)
    scratch = [
        pltpu.VMEM((1, ROWS, TOKENS, C), BF16),
        pltpu.VMEM((HEADS, slice_rows), BF16),
        pltpu.VMEM((C, C), F32),
        pltpu.VMEM((slice_rows, 4 * C), BF16),
        pltpu.VMEM((PARTS, slice_rows, C), BF16),
        pltpu.VMEM((2, slice_rows, FF), BF16),
        pltpu.VMEM((PARTS, dp_count, slice_rows, C), BF16),
        pltpu.VMEM((2, dp_count, slice_rows, FF), BF16),
        pltpu.VMEM((2, dp_count, slice_rows, FF), BF16),
        pltpu.VMEM((2, dp_count, FF // dp_count // 2, C), BF16),
        pltpu.VMEM((PARTS, C, C), BF16),
        pltpu.VMEM((8, C, C), BF16),
        pltpu.VMEM((2 * FF, C), BF16),
        pltpu.VMEM((C, FF), BF16),
        pltpu.VMEM((DAP, 64, C), BF16),
        pltpu.VMEM((DAP, 64, C), BF16),
        pltpu.VMEM((ROWS, TOKENS, C), BF16),
        pltpu.VMEM((2, 2, PART * ROWS, 128), F32),
        pltpu.VMEM((PARTS, DAP, 16, TOKENS), BF16),
        pltpu.VMEM((PARTS, DAP, 16, TOKENS), BF16),
        pltpu.VMEM((PARTS, DAP, 16, 128), BF16),
        pltpu.VMEM((PARTS, DAP, 16, 128), BF16),
        pltpu.VMEM((2, C * ROWS, 128), F32),
        pltpu.VMEM((ROWS, TOKENS), F32),
        pltpu.VMEM((ROWS, TOKENS), F32),
        pltpu.VMEM((TOKENS * ROWS, C), F32),
        pltpu.VMEM((ROWS, C, TOKENS), F32),
        pltpu.VMEM((ROWS, C, TOKENS), F32),
        pltpu.VMEM((ROWS, C, TOKENS), F32),
        pltpu.VMEM((ROWS, C, TOKENS), BF16),
        pltpu.VMEM((2, 2, 8 * GROUP, 128), F32),
        pltpu.VMEM((2, HEADS * GROUP, TOKENS), BF16),
        pltpu.VMEM((2, 2, DAP // 2, HEADS * GROUP, TOKENS), BF16),
        pltpu.VMEM((TOKENS, HEADS * TOKENS), F32),
        pltpu.VMEM((ROWS, C, HEADS * TOKENS), BF16),
        pltpu.VMEM((ROWS, TOKENS, C), BF16),
        pltpu.VMEM((ROWS, HEADS, 48, TOKENS), BF16),
        pltpu.VMEM((ROWS, C, TOKENS), F32),
        pltpu.VMEM((ROWS, TOKENS, HEADS * TOKENS), F32),
        pltpu.VMEM((2, C, TOKENS), F32),
        pltpu.VMEM((ROWS // 2, DAP, 16, C), BF16),
        pltpu.SemaphoreType.DMA((4 + PARTS,)),
        pltpu.SemaphoreType.DMA((4 + PARTS,)),
        pltpu.SemaphoreType.DMA((4,)),
        pltpu.SemaphoreType.DMA((4,)),
        pltpu.SemaphoreType.DMA((2,)),
        pltpu.SemaphoreType.DMA((PARTS,)),
        pltpu.SemaphoreType.DMA((PARTS,)),
        pltpu.SemaphoreType.DMA((PARTS,)),
        pltpu.SemaphoreType.DMA((PARTS,)),
        pltpu.SemaphoreType.DMA((2,)),
        pltpu.SemaphoreType.DMA((2,)),
        pltpu.SemaphoreType.DMA((2,)),
        pltpu.SemaphoreType.DMA((2,)),
        pltpu.SemaphoreType.DMA((ROWS // 2,)),
        pltpu.SemaphoreType.DMA((ROWS // 2,)),
        pltpu.SemaphoreType.DMA((8,)),
        pltpu.SemaphoreType.REGULAR,
    ]
    blocks = pl.pallas_call(
        functools.partial(body, dp_count),
        out_shape=jax.ShapeDtypeStruct((ROWS // 2, DAP, 16, C), BF16),
        in_specs=[pl.BlockSpec(memory_space=pltpu.SMEM)] + [anywhere] * 9,
        out_specs=anywhere,
        scratch_shapes=scratch,
        compiler_params=pltpu.CompilerParams(
            collective_id=0, has_side_effects=True, vmem_limit_bytes=VMEM_LIMIT
        ),
    )(lengths, pair_repr, *weights[:4], jnp.transpose(weights[4]), *weights[5:])
    return pl.pallas_call(
        to_rows,
        out_shape=jax.ShapeDtypeStruct((1, ROWS, TOKENS, C), BF16),
        in_specs=[anywhere],
        out_specs=anywhere,
        scratch_shapes=[
            pltpu.VMEM((ROWS // 2, DAP, 16, C), BF16),
            pltpu.VMEM((DAP, 64, C), F32),
            pltpu.VMEM((ROWS, TOKENS, C), BF16),
            pltpu.SemaphoreType.DMA((ROWS // 2,)),
            pltpu.SemaphoreType.DMA((ROWS,)),
        ],
        compiler_params=pltpu.CompilerParams(vmem_limit_bytes=VMEM_LIMIT),
    )(blocks)


def solution(mesh):
    dp_count = mesh.shape["dp"]
    placed = (P("dp", "dap", None, None), P("dp")) + (P("dp", None),) * 8
    return jax.shard_map(
        functools.partial(fused, dp_count),
        mesh=mesh,
        in_specs=placed,
        out_specs=P("dp", "dap", None, None),
        check_vma=False,
    )
```

```python
import functools

import jax
import jax.numpy as jnp
from jax import lax
from jax.experimental import pallas as pl
from jax.experimental.pallas import tpu as pltpu
from jax.sharding import PartitionSpec as P

F32 = jnp.float32
BF16 = jnp.bfloat16
NN = (((1,), (0,)), ((), ()))
NT = (((1,), (1,)), ((), ()))
TN = (((0,), (0,)), ((), ()))
LOG2E = 1.4426950408889634
EPS = 1e-05

ROWS = 8
TOKENS = 256
C = 128
HEADS = 4
HEAD = 32
FF = 512
VMEM_LIMIT = 64 * 1024 * 1024 - 65536
DAP = TOKENS // ROWS
PARTS = 4
PART = C // PARTS
GROUP = ROWS // 2


OFFSETS = (
    (2, 2), (2, 3), (3, 2), (2, 1), (1, 2), (0, 2), (2, 0), (3, 1),
    (1, 3), (3, 3), (1, 1), (0, 3), (3, 0), (0, 1), (1, 0),
)
MESH = pl.DeviceIdType.MESH


def dot(left, right, dims):
    return lax.dot_general(left, right, dims, preferred_element_type=F32)


def sigmoid(v):
    return 0.5 + 0.5 * jnp.tanh(0.5 * v)


def norm_over(values, axis):
    mean = jnp.mean(values, axis=axis, keepdims=True)
    centred = values - mean
    variance = jnp.mean(centred * centred, axis=axis, keepdims=True)
    return centred * lax.rsqrt(variance + EPS)


def transposed(value):
    return jnp.transpose(value.astype(F32)).astype(BF16)


def wait_bytes(ref, sem):
    pltpu.make_async_copy(ref, ref, sem).wait()


def body(
    dp_count,
    length_ref,
    x_hbm,
    tri_project_ref,
    tri_gate_ref,
    tri_output_ref,
    attn_project_ref,
    attn_bias_ref,
    attn_output_ref,
    expand_ref,
    reduce_ref,
    out_recv,
    x_ref,
    bias_in,
    bias_square,
    tri_in,
    tri_stage,
    mix_stage,
    w_tri,
    w_mix,
    w_expand,
    w_reduce,
    wt_tri,
    wt_mix,
    wt_expand,
    wt_reduce,
    pair_stage,
    pair_recv,
    normed_rows,
    lr_rows,
    lr_stage,
    lr_recv,
    c_stage,
    c_recv,
    c_values,
    c_mean,
    c_scale,
    x_cols,
    xt,
    gate_t,
    first_t,
    first_norm_t,
    bias_rows,
    bias_stage,
    bias_recv,
    bias_t,
    q_diag,
    k_cols,
    v_aug,
    og_t,
    scores_ref,
    second_t,
    unit,
    out_stage,
    w_send,
    w_recv,
    relay_send,
    relay_recv,
    pair_sems,
    lr_send,
    lr_recv_sem,
    c_send,
    c_recv_sem,
    bias_send,
    bias_recv_sem,
    bias_relay_send,
    bias_relay_recv,
    out_send,
    out_recv_sem,
    load_sems,
    ready_sem,
):
    me = lax.axis_index("dap")
    my_dp = lax.axis_index("dp")
    core = me % 2
    my_chip = me // 2
    chip_x = (me // 2) % 4
    chip_y = me // 8

    sibling = me + 1 - 2 * core

    def chip_of(off_x, off_y):
        return (chip_y + off_y) % 4 * 4 + (chip_x + off_x) % 4

    peers = []
    same_core = []
    unheard = []
    for off_x, off_y in OFFSETS:
        chip = chip_of(off_x, off_y)
        both = [chip * 2 + core, chip * 2 + 1 - core]
        peers += both
        same_core += both[:1]
        if off_y != 0:
            unheard += both if off_x != 0 else both[1:]
    peers.append(sibling)

    def send_blocks(targets, stage, recv, send_sem, recv_sem):
        for target in targets:
            pltpu.make_async_remote_copy(
                src_ref=stage.at[target],
                dst_ref=recv.at[me],
                send_sem=send_sem,
                recv_sem=recv_sem,
                device_id={"dap": target},
                device_id_type=MESH,
            ).start()

    pending = []

    def exchange(stage, recv, send_sem, recv_sem):
        send_blocks(peers, stage, recv, send_sem, recv_sem)
        pltpu.make_async_copy(stage.at[me], recv.at[me], recv_sem).start()
        pending.append((stage.at[pl.ds(0, DAP - 1)], send_sem))

    def weight_sends(source, dest, index):
        def send(step, carry):
            target = (my_dp + step) % dp_count
            pltpu.make_async_remote_copy(
                src_ref=source,
                dst_ref=dest.at[my_dp],
                send_sem=w_send.at[index],
                recv_sem=w_recv.at[index],
                device_id={"dp": target},
                device_id_type=MESH,
            ).start()
            return carry

        lax.fori_loop(1, dp_count, send, 0)
        pltpu.make_async_copy(source, dest.at[my_dp], w_recv.at[index]).start()
        pending.append((dest.at[pl.ds(0, dp_count - 1)], w_send.at[index]))

    load_x = pltpu.make_async_copy(x_hbm, x_ref, load_sems.at[0])
    load_x.start()
    load_tri = pltpu.make_async_copy(tri_project_ref, tri_in, load_sems.at[7])
    load_tri.start()
    loads = [
        pltpu.make_async_copy(tri_gate_ref, mix_stage.at[0, :, 0:128], load_sems.at[1]),
        pltpu.make_async_copy(tri_output_ref, mix_stage.at[0, :, 128:256], load_sems.at[2]),
        pltpu.make_async_copy(
            attn_project_ref.at[:, 0:256], mix_stage.at[0, :, 256:512], load_sems.at[3]
        ),
        pltpu.make_async_copy(
            attn_project_ref.at[:, 256:512], mix_stage.at[1, :, 0:256], load_sems.at[6]
        ),
        pltpu.make_async_copy(attn_output_ref, mix_stage.at[1, :, 256:384], load_sems.at[4]),
        pltpu.make_async_copy(attn_bias_ref, bias_in, load_sems.at[5]),
    ]
    for load in loads:
        load.start()

    def relay(weights, index):
        wait_bytes(weights.at[0], w_recv.at[index])
        pltpu.make_async_remote_copy(
            src_ref=weights.at[core],
            dst_ref=weights.at[core],
            send_sem=relay_send.at[index],
            recv_sem=relay_recv.at[index],
            device_id={"dap": sibling},
            device_id_type=MESH,
        ).start()
        pending.append((weights.at[0], relay_send.at[index]))

    barrier = pltpu.get_barrier_semaphore()

    for step in range(1, dp_count):
        pl.semaphore_signal(
            barrier,
            inc=1,
            device_id={"dp": (my_dp + step) % dp_count},
            device_id_type=MESH,
        )
    column_chips = [chip_of(0, off) * 2 + core for off in (2, 1, 3)]
    row_group = []
    for off in (2, 1, 3):
        row_group += [chip_of(off, 0) * 2 + core, chip_of(off, 0) * 2 + 1 - core]
    for target in column_chips + row_group + [sibling]:
        pl.semaphore_signal(barrier, inc=1, device_id={"dap": target}, device_id_type=MESH)

    load_tri.wait()
    tri_whole = tri_in[...].astype(F32)
    for quarter in range(PARTS):
        tri_stage[quarter] = jnp.concatenate(
            [
                tri_whole[:, part * C + quarter * PART : part * C + (quarter + 1) * PART]
                for part in range(4)
            ],
            axis=1,
        ).astype(BF16)

    load_x.wait()

    def cut_pair(two, carry):
        start = pl.multiple_of(two * 16, 16)
        both = x_ref[0, :, pl.ds(start, 16), :].astype(F32)
        pair_stage[two * 2] = both[:, :8].reshape(64, C).astype(BF16)
        pair_stage[two * 2 + 1] = both[:, 8:].reshape(64, C).astype(BF16)
        return carry

    lax.fori_loop(0, DAP // 2, cut_pair, 0, unroll=2)

    def norm_row(row, carry):
        normed_rows[row] = norm_over(x_ref[0, row].astype(F32), 1).astype(BF16)
        return carry

    lax.fori_loop(0, ROWS, norm_row, 0, unroll=2)
    pl.semaphore_wait(barrier, dp_count - 1 + 10)

    for target in column_chips:
        pl.semaphore_signal(ready_sem, inc=1, device_id={"dap": target}, device_id_type=MESH)
    weight_sends(tri_stage.at[0], w_tri.at[0], 4)
    heard = row_group + column_chips + [sibling]
    send_blocks(heard, pair_stage, pair_recv, pair_sems.at[0], pair_sems.at[1])

    for quarter in range(1, PARTS):
        weight_sends(tri_stage.at[quarter], w_tri.at[quarter], 4 + quarter)
    pl.semaphore_wait(ready_sem, 3)
    send_blocks(unheard, pair_stage, pair_recv, pair_sems.at[0], pair_sems.at[1])
    pltpu.make_async_copy(pair_stage.at[me], pair_recv.at[me], pair_sems.at[1]).start()
    pending.append((pair_stage.at[pl.ds(0, DAP - 1)], pair_sems.at[0]))

    length = length_ref[0]
    valid_cols = (lax.broadcasted_iota(jnp.int32, (1, TOKENS), 1) < length).astype(F32)

    for quarter in range(PARTS):
        wait_bytes(w_tri.at[quarter], w_recv.at[4 + quarter])
        wt_tri[quarter] = transposed(w_tri[quarter].reshape(C, C))

        def project_row(row, carry):
            valid_row = (me * ROWS + row < length).astype(F32)
            mask = valid_cols * valid_row
            projected = dot(wt_tri[quarter], normed_rows[row], NT)
            for side in range(2):
                gate = projected[2 * side * PART : (2 * side + 1) * PART]
                value = projected[(2 * side + 1) * PART : (2 * side + 2) * PART]
                kept = sigmoid(gate) * value * mask
                lr_rows[side, 0, pl.ds(row, PART, stride=ROWS), :] = kept[:, :128]
                lr_rows[side, 1, pl.ds(row, PART, stride=ROWS), :] = kept[:, 128:]
            return carry

        lax.fori_loop(0, ROWS, project_row, 0, unroll=8)
        for lanes in range(2):
            lr_stage[quarter, :, :, lanes * 128 : (lanes + 1) * 128] = jnp.concatenate(
                [lr_rows[side, lanes].reshape(DAP, ROWS, 128) for side in range(2)], axis=1
            ).astype(BF16)
        exchange(
            lr_stage.at[quarter],
            lr_recv.at[quarter],
            lr_send.at[quarter],
            lr_recv_sem.at[quarter],
        )
        if quarter > 0:
            continue

        for load in loads:
            load.wait()
        slice_rows = mix_stage.shape[1]
        bias_square[...] = jnp.zeros((C, C), F32)
        bias_square[0:HEADS, 0:slice_rows] = bias_in[...].astype(F32)
        mix_stage[1, :, 384:512] = jnp.transpose(bias_square[...])[0:slice_rows].astype(BF16)
        lanes = pl.ds(pl.multiple_of(core * FF, FF), FF)
        rows_sent = reduce_ref.shape[0] // 2
        rows = pl.ds(pl.multiple_of(core * rows_sent, rows_sent), rows_sent)
        weight_sends(mix_stage.at[core], w_mix.at[core], 1)
        weight_sends(expand_ref.at[:, lanes], w_expand.at[core], 2)
        weight_sends(reduce_ref.at[rows, :], w_reduce.at[core], 3)

    relay(w_mix, 1)
    wait_bytes(pair_recv, pair_sems.at[1])
    x_cols[...] = pair_recv[...].astype(F32).reshape(TOKENS * ROWS, C)

    wait_bytes(w_mix.at[0], relay_recv.at[1])
    for part in range(8):
        wt_mix[part] = transposed(
            w_mix[part // 4, :, :, (part % 4) * C : (part % 4 + 1) * C].reshape(C, C)
        )

    def column_gate(col, carry):
        column = jnp.transpose(x_cols[pl.ds(col, TOKENS, stride=ROWS), :])
        xt[col] = column
        normed = norm_over(column, 0).astype(BF16)
        gate_t[col] = sigmoid(dot(wt_mix[0], normed, NN))
        return carry

    lax.fori_loop(0, ROWS, column_gate, 0, unroll=4)
    v_aug[...] = jnp.ones(v_aug.shape, BF16)
    q_diag[...] = jnp.zeros(q_diag.shape, BF16)

    for quarter in range(PARTS):
        wait_bytes(lr_recv.at[quarter], lr_recv_sem.at[quarter])
        both = lr_recv[quarter].astype(F32)
        left = both[:, :ROWS].reshape(TOKENS, TOKENS).astype(BF16)
        right = both[:, ROWS:].reshape(TOKENS, TOKENS).astype(BF16)
        total = dot(right, left, NT)
        c_stage[quarter] = jnp.concatenate(
            [
                total[:, :128].reshape(DAP, ROWS, 128),
                total[:, 128:].reshape(DAP, ROWS, 128),
            ],
            axis=1,
        ).astype(BF16)
        exchange(
            c_stage.at[quarter],
            c_recv.at[quarter],
            c_send.at[quarter],
            c_recv_sem.at[quarter],
        )
        if quarter == 1:
            relay(w_expand, 2)
        if quarter == 2:
            relay(w_reduce, 3)

    wait_bytes(w_expand.at[0], relay_recv.at[2])
    for part in range(8):
        wt_expand[part * C : (part + 1) * C] = transposed(
            w_expand[part // 4, :, :, (part % 4) * C : (part % 4 + 1) * C].reshape(C, C)
        )
    wait_bytes(w_reduce.at[0], relay_recv.at[3])
    blocks = [(half, index) for index in range(dp_count) for half in range(2)]
    for part in range(FF // C):
        own = blocks[part * len(blocks) * C // FF : (part + 1) * len(blocks) * C // FF]
        wt_reduce[:, part * C : (part + 1) * C] = transposed(
            jnp.concatenate([w_reduce[half, index] for half, index in own], axis=0)
        )

    means = []
    squares = []
    zero = jnp.zeros((16, 128), F32)
    for quarter in range(PARTS):
        wait_bytes(c_recv.at[quarter], c_recv_sem.at[quarter])

        def c_sum(step, total):
            for inner in range(4):
                block = step * 4 + inner
                value = c_recv[quarter, block].astype(F32)
                start = pl.multiple_of((quarter * PART + block) * ROWS, ROWS)
                c_values[0, pl.ds(start, ROWS), :] = value[:ROWS]
                c_values[1, pl.ds(start, ROWS), :] = value[ROWS:]
                total = total + value
            return total

        mean = lax.fori_loop(0, PART // 4, c_sum, zero) * (1.0 / PART)

        def c_square(step, total):
            for inner in range(4):
                apart = c_recv[quarter, step * 4 + inner].astype(F32) - mean
                total = total + apart * apart
            return total

        means.append(mean)
        squares.append(lax.fori_loop(0, PART // 4, c_square, zero))
    mean = sum(means) * (1.0 / PARTS)
    variance = sum(
        square + (own - mean) * (own - mean) * PART for square, own in zip(squares, means)
    ) * (1.0 / C)
    scale = lax.rsqrt(variance + EPS)
    c_mean[...] = jnp.concatenate([mean[:ROWS], mean[ROWS:]], axis=1)
    c_scale[...] = jnp.concatenate([scale[:ROWS], scale[ROWS:]], axis=1)

    def column_first(col, carry):
        values = jnp.concatenate(
            [
                c_values[0, pl.ds(col, C, stride=ROWS), :],
                c_values[1, pl.ds(col, C, stride=ROWS), :],
            ],
            axis=1,
        )
        normed = ((values - c_mean[pl.ds(col, 1), :]) * c_scale[pl.ds(col, 1), :]).astype(BF16)
        first = xt[col] + gate_t[col] * dot(wt_mix[1], normed, NN)
        first_t[col] = first
        first_norm = norm_over(first, 0).astype(BF16)
        first_norm_t[col] = first_norm
        bias = dot(wt_mix[7, 0:16], first_norm, NN)[:8]
        slot = col // GROUP
        inner = col - slot * GROUP
        bias_rows[slot, 0, pl.ds(inner, 8, stride=GROUP), :] = bias[:, :128]
        bias_rows[slot, 1, pl.ds(inner, 8, stride=GROUP), :] = bias[:, 128:]
        return carry

    for half in range(2):
        lax.fori_loop(half * GROUP, (half + 1) * GROUP, column_first, 0, unroll=4)
        for lanes in range(2):
            bias_stage[half, :, lanes * 128 : (lanes + 1) * 128] = bias_rows[
                half, lanes, 0 : HEADS * GROUP
            ].astype(BF16)
        for target in same_core:
            pltpu.make_async_remote_copy(
                src_ref=bias_stage.at[half],
                dst_ref=bias_recv.at[half, core, my_chip],
                send_sem=bias_send.at[half],
                recv_sem=bias_recv_sem.at[half],
                device_id={"dap": target},
                device_id_type=MESH,
            ).start()
        pltpu.make_async_copy(
            bias_stage.at[half], bias_recv.at[half, core, my_chip], bias_recv_sem.at[half]
        ).start()
        pending.append((bias_recv.at[half, 0, pl.ds(0, DAP // 2 - 1)], bias_send.at[half]))

    def relay_bias(half):
        wait_bytes(bias_recv.at[half, 0], bias_recv_sem.at[half])
        pltpu.make_async_remote_copy(
            src_ref=bias_recv.at[half, core],
            dst_ref=bias_recv.at[half, core],
            send_sem=bias_relay_send.at[half],
            recv_sem=bias_relay_recv.at[half],
            device_id={"dap": sibling},
            device_id_type=MESH,
        ).start()
        pending.append((bias_recv.at[half, 0], bias_relay_send.at[half]))

    q_scale = LOG2E / HEAD**0.5

    def column_project(col, carry):
        first_norm = first_norm_t[col]
        query = (dot(wt_mix[2], first_norm, NN) * q_scale).astype(BF16)
        value = dot(wt_mix[4], first_norm, NN).astype(BF16)
        og_t[col] = sigmoid(dot(wt_mix[5], first_norm, NN))
        k_cols[col] = transposed(dot(wt_mix[3], first_norm, NN))
        for head in range(HEADS):
            rows = slice(head * HEAD, (head + 1) * HEAD)
            q_diag[col, rows, head * TOKENS : (head + 1) * TOKENS] = query[rows]
            v_aug[col, head, 0:HEAD, :] = value[rows]
        return carry

    lax.fori_loop(0, ROWS, column_project, 0, unroll=4)

    relay_bias(0)
    unit[...] = (
        lax.broadcasted_iota(jnp.int32, (TOKENS, TOKENS), 0)
        == lax.broadcasted_iota(jnp.int32, (TOKENS, TOKENS), 1)
    ).astype(F32).astype(BF16)

    def column_scores(col, carry):
        for head in range(HEADS):
            lanes = slice(head * TOKENS, (head + 1) * TOKENS)
            scores_ref[col, :, lanes] = dot(k_cols[col], q_diag[col, :, lanes], NN)
        return carry

    lax.fori_loop(0, ROWS, column_scores, 0, unroll=4)
    relay_bias(1)
    for half in range(2):
        wait_bytes(bias_recv.at[half, 0], bias_relay_recv.at[half])
    masked = jnp.where(
        lax.broadcasted_iota(jnp.int32, (TOKENS, TOKENS), 0) < length, 0.0, -1e9
    )
    for pair in range(HEADS // 2):
        tiles = []
        for half in range(2):
            by_core = bias_recv[half].astype(F32)[:, :, pair * 8 : pair * 8 + 8]
            by_chip = [by_core[own, chip] for chip in range(DAP // 2) for own in range(2)]
            tiles.append(jnp.stack(by_chip, axis=0))
        low = lax.broadcasted_iota(jnp.int32, (DAP, 8, TOKENS), 1) < GROUP
        swapped = [pltpu.roll(tile, GROUP, 1) for tile in tiles]
        heads = (
            jnp.where(low, tiles[0], swapped[1]),
            jnp.where(low, swapped[0], tiles[1]),
        )
        for inner in range(2):
            turned = dot(unit[...], heads[inner].reshape(TOKENS, TOKENS).astype(BF16), NT)
            head = pair * 2 + inner
            bias_t[:, head * TOKENS : (head + 1) * TOKENS] = turned * LOG2E + masked

    def attend(two):
        seconds = []
        for col in (two * 2, two * 2 + 1):
            scores = [
                scores_ref[col, :, head * TOKENS : (head + 1) * TOKENS]
                + bias_t[:, head * TOKENS : (head + 1) * TOKENS]
                for head in range(HEADS)
            ]
            softs = [
                jnp.exp2(score - jnp.max(score, axis=0, keepdims=True)).astype(BF16)
                for score in scores
            ]
            sums = [dot(v_aug[col, head], softs[head], NN) for head in range(HEADS)]
            attended = jnp.concatenate(
                [total[0:HEAD] * (1.0 / total[HEAD : HEAD + 1]) for total in sums], axis=0
            )
            gated = (attended * og_t[col]).astype(BF16)
            seconds.append(first_t[col] + dot(wt_mix[6], gated, NN))
        return seconds

    def transition(seconds):
        norms = [norm_over(second, 0).astype(BF16) for second in seconds]
        hiddens = [dot(wt_expand[0:FF], norm, NN) for norm in norms]
        ups = [dot(wt_expand[FF : 2 * FF], norm, NN) for norm in norms]
        activated = [
            (hidden * sigmoid(hidden) * up).astype(BF16) for hidden, up in zip(hiddens, ups)
        ]
        results = [
            jnp.transpose(second + dot(wt_reduce[...], act, NN)).reshape(-1, ROWS, C)
            for second, act in zip(seconds, activated)
        ]
        return jnp.concatenate(results, axis=1).astype(BF16)

    def send_out(two):
        exchange(out_stage.at[two], out_recv.at[two], out_send.at[two], out_recv_sem.at[two])
        pending.pop()

    second_t[0], second_t[1] = attend(0)

    def column_attend(two, carry):
        before = [second_t[0], second_t[1]]
        out_stage[two - 1] = transition(before)
        after = attend(two)
        send_out(two - 1)
        second_t[0], second_t[1] = after
        return carry

    lax.fori_loop(1, ROWS // 2, column_attend, 0, unroll=3)
    last = ROWS // 2 - 1
    for half in range(2):
        owners = DAP // 2
        lanes = slice(half * 128, (half + 1) * 128)
        out_stage[last, half * owners : (half + 1) * owners] = transition(
            [second_t[0, :, lanes], second_t[1, :, lanes]]
        )
        targets = [half * owners + (me + step) % owners for step in range(owners)]
        send_blocks(
            targets[1:],
            out_stage.at[last],
            out_recv.at[last],
            out_send.at[last],
            out_recv_sem.at[last],
        )

        @pl.when(me // owners != half)
        def _():
            send_blocks(
                targets[:1],
                out_stage.at[last],
                out_recv.at[last],
                out_send.at[last],
                out_recv_sem.at[last],
            )

    pltpu.make_async_copy(
        out_stage.at[last, me], out_recv.at[last, me], out_recv_sem.at[last]
    ).start()

    for two in range(ROWS // 2):
        wait_bytes(out_recv.at[two], out_recv_sem.at[two])

    for two in range(ROWS // 2):
        wait_bytes(out_stage.at[two, pl.ds(0, DAP - 1)], out_send.at[two])
    for ref, sem in pending:
        wait_bytes(ref, sem)


def to_rows(blocks_ref, out_ref, blocks, wide, rows, load_sems, store_sems):
    loads = [
        pltpu.make_async_copy(blocks_ref.at[two], blocks.at[two], load_sems.at[two])
        for two in range(ROWS // 2)
    ]
    for load in loads:
        load.start()
    for two, load in enumerate(loads):
        load.wait()
        wide[:, two * 16 : (two + 1) * 16] = blocks[two].astype(F32)
    flat = wide.reshape(TOKENS * ROWS, C)
    stores = []
    for row in range(ROWS):
        rows[row] = flat[pl.ds(row, TOKENS, stride=ROWS), :].astype(BF16)
        stores.append(pltpu.make_async_copy(rows.at[row], out_ref.at[0, row], store_sems.at[row]))
        stores[-1].start()
    for store in stores:
        store.wait()


def fused(dp_count, pair_repr, lengths, *weights):
    slice_rows = C // dp_count
    anywhere = pl.BlockSpec(memory_space=pltpu.HBM)
    scratch = [
        pltpu.VMEM((1, ROWS, TOKENS, C), BF16),
        pltpu.VMEM((HEADS, slice_rows), BF16),
        pltpu.VMEM((C, C), F32),
        pltpu.VMEM((slice_rows, 4 * C), BF16),
        pltpu.VMEM((PARTS, slice_rows, C), BF16),
        pltpu.VMEM((2, slice_rows, FF), BF16),
        pltpu.VMEM((PARTS, dp_count, slice_rows, C), BF16),
        pltpu.VMEM((2, dp_count, slice_rows, FF), BF16),
        pltpu.VMEM((2, dp_count, slice_rows, FF), BF16),
        pltpu.VMEM((2, dp_count, FF // dp_count // 2, C), BF16),
        pltpu.VMEM((PARTS, C, C), BF16),
        pltpu.VMEM((8, C, C), BF16),
        pltpu.VMEM((2 * FF, C), BF16),
        pltpu.VMEM((C, FF), BF16),
        pltpu.VMEM((DAP, 64, C), BF16),
        pltpu.VMEM((DAP, 64, C), BF16),
        pltpu.VMEM((ROWS, TOKENS, C), BF16),
        pltpu.VMEM((2, 2, PART * ROWS, 128), F32),
        pltpu.VMEM((PARTS, DAP, 16, TOKENS), BF16),
        pltpu.VMEM((PARTS, DAP, 16, TOKENS), BF16),
        pltpu.VMEM((PARTS, DAP, 16, 128), BF16),
        pltpu.VMEM((PARTS, DAP, 16, 128), BF16),
        pltpu.VMEM((2, C * ROWS, 128), F32),
        pltpu.VMEM((ROWS, TOKENS), F32),
        pltpu.VMEM((ROWS, TOKENS), F32),
        pltpu.VMEM((TOKENS * ROWS, C), F32),
        pltpu.VMEM((ROWS, C, TOKENS), F32),
        pltpu.VMEM((ROWS, C, TOKENS), F32),
        pltpu.VMEM((ROWS, C, TOKENS), F32),
        pltpu.VMEM((ROWS, C, TOKENS), BF16),
        pltpu.VMEM((2, 2, 8 * GROUP, 128), F32),
        pltpu.VMEM((2, HEADS * GROUP, TOKENS), BF16),
        pltpu.VMEM((2, 2, DAP // 2, HEADS * GROUP, TOKENS), BF16),
        pltpu.VMEM((TOKENS, HEADS * TOKENS), F32),
        pltpu.VMEM((ROWS, C, HEADS * TOKENS), BF16),
        pltpu.VMEM((ROWS, TOKENS, C), BF16),
        pltpu.VMEM((ROWS, HEADS, 48, TOKENS), BF16),
        pltpu.VMEM((ROWS, C, TOKENS), F32),
        pltpu.VMEM((ROWS, TOKENS, HEADS * TOKENS), F32),
        pltpu.VMEM((2, C, TOKENS), F32),
        pltpu.VMEM((TOKENS, TOKENS), BF16),
        pltpu.VMEM((ROWS // 2, DAP, 16, C), BF16),
        pltpu.SemaphoreType.DMA((4 + PARTS,)),
        pltpu.SemaphoreType.DMA((4 + PARTS,)),
        pltpu.SemaphoreType.DMA((4,)),
        pltpu.SemaphoreType.DMA((4,)),
        pltpu.SemaphoreType.DMA((2,)),
        pltpu.SemaphoreType.DMA((PARTS,)),
        pltpu.SemaphoreType.DMA((PARTS,)),
        pltpu.SemaphoreType.DMA((PARTS,)),
        pltpu.SemaphoreType.DMA((PARTS,)),
        pltpu.SemaphoreType.DMA((2,)),
        pltpu.SemaphoreType.DMA((2,)),
        pltpu.SemaphoreType.DMA((2,)),
        pltpu.SemaphoreType.DMA((2,)),
        pltpu.SemaphoreType.DMA((ROWS // 2,)),
        pltpu.SemaphoreType.DMA((ROWS // 2,)),
        pltpu.SemaphoreType.DMA((8,)),
        pltpu.SemaphoreType.REGULAR,
    ]
    blocks = pl.pallas_call(
        functools.partial(body, dp_count),
        out_shape=jax.ShapeDtypeStruct((ROWS // 2, DAP, 16, C), BF16),
        in_specs=[pl.BlockSpec(memory_space=pltpu.SMEM)] + [anywhere] * 9,
        out_specs=anywhere,
        scratch_shapes=scratch,
        compiler_params=pltpu.CompilerParams(
            collective_id=0, has_side_effects=True, vmem_limit_bytes=VMEM_LIMIT
        ),
    )(lengths, pair_repr, *weights[:4], jnp.transpose(weights[4]), *weights[5:])
    return pl.pallas_call(
        to_rows,
        out_shape=jax.ShapeDtypeStruct((1, ROWS, TOKENS, C), BF16),
        in_specs=[anywhere],
        out_specs=anywhere,
        scratch_shapes=[
            pltpu.VMEM((ROWS // 2, DAP, 16, C), BF16),
            pltpu.VMEM((DAP, 64, C), F32),
            pltpu.VMEM((ROWS, TOKENS, C), BF16),
            pltpu.SemaphoreType.DMA((ROWS // 2,)),
            pltpu.SemaphoreType.DMA((ROWS,)),
        ],
        compiler_params=pltpu.CompilerParams(vmem_limit_bytes=VMEM_LIMIT),
    )(blocks)


def solution(mesh):
    dp_count = mesh.shape["dp"]
    placed = (P("dp", "dap", None, None), P("dp")) + (P("dp", None),) * 8
    return jax.shard_map(
        functools.partial(fused, dp_count),
        mesh=mesh,
        in_specs=placed,
        out_specs=P("dp", "dap", None, None),
        check_vma=False,
    )
```
